256 devices in a mesh: row: 8 (over z), col: 8 (over x, core), sub: 4 (over y).
Axes of the slice: x: 4, y: 4, z: 8, core: 2. Of those that a mesh axis runs over, the one named last changes fastest.
Arguments:
- front: float32 [12288, 12288], P('row', ('col', 'sub')), as said below
- bases: float32 [12288, 128], P('row'), may hold values from -1 to 1, as said below
- ranks: int32 [96, 4], replicated, may hold values from 8 to 32
- child_map: int32 [4, 32], replicated, may hold values from 0 to 95, as said below
- child_factors: float32 [4, 4096, 128], P('sub', ('row', 'col')), may hold values from -2.1 to 2.1
- child_weights: float32 [4, 128], replicated, may hold values from 0.1 to 1
Outputs:
- front_out: float32 [12288, 12288], P('row', ('col', 'sub'))
- factors: float32 [12288, 128], P('row')
- pivots: float32 [512], replicated
The draws below stay inside these ranges and needn't reach their ends.
Inputs may be any that keep to these rules, and one draw needn't show every extreme that they name: `child_map`: within one child the 32 block numbers are distinct. `front`: symmetric positive definite, with a large positive diagonal (about 1.5 to 2.5 times sqrt(12288)). `bases`: each 128 x 32 block has orthonormal columns.
All inputs are finite; a program needn't handle non-finite values.
Results may differ from the reference program's by a relative error of at most 0.0001.
Values sent between devices are 32-bit elements; how exact they have to be, the bound alone decides.
A program may use at most 128 MiB of HBM per device.

```python
import math
import jax
import jax.numpy as jnp
from jax import lax

BS = 128
NF = 12288
NP = 4
RMAX = 32
RLO = 8
NC = 4096
RC = 128
NBLK = 96
NCB = 32
CHILDREN = 4


def draw_front(key, part):
    key = jax.random.fold_in(key, 11)
    first_key, second_key = jax.random.split(key)
    raw = jax.random.normal(first_key, (NF, NF), jnp.float32) * 0.5
    symmetric = (raw + raw.T) * 0.7071
    diagonal = jax.random.uniform(second_key, (NF,), jnp.float32, 1.5, 2.5) * math.sqrt(NF)
    places = jnp.arange(NF, dtype=jnp.int32)
    return symmetric.at[places, places].add(diagonal)


def draw_bases(key, part):
    key = jax.random.fold_in(key, 37)
    vector = jax.random.normal(key, (NBLK, NP, BS), jnp.float32)
    weight = jnp.where(jnp.arange(BS, dtype=jnp.int32) < RMAX, jnp.float32(3.0), jnp.float32(1.0))
    vector = vector * weight[None, None, :]
    length = jnp.sum(vector * vector, axis=-1)
    unit = jnp.eye(BS, RMAX, dtype=jnp.float32)
    blocks = unit[None, None, :, :] - 2.0 * vector[:, :, :, None] * vector[:, :, None, :RMAX] / length[:, :, None, None]
    return jnp.transpose(blocks, (0, 2, 1, 3)).reshape(NF, NP * RMAX)


def draw_child_map(key, part):
    key = jax.random.fold_in(key, 23)
    order = jax.random.permutation(key, NBLK).astype(jnp.int32)
    places = (jnp.arange(CHILDREN, dtype=jnp.int32)[:, None] * NCB + jnp.arange(NCB, dtype=jnp.int32)[None, :]) % NBLK
    return order[places].astype(jnp.int32)


def with_ends(array, rng, low, high):
    dims = array.shape
    place = [jax.random.randint(jax.random.fold_in(rng, axis), (), 0, dims[axis]) for axis in range(len(dims))]
    array = array.at[tuple(place)].set(low)
    longest = dims.index(max(dims))
    place[longest] = (place[longest] + 1) % dims[longest]
    return array.at[tuple(place)].set(high)


def shard_levels(own_key, dims, pieces, low, high):
    def one(dim, parts):
        steps = jax.random.uniform(jax.random.fold_in(jax.random.fold_in(own_key, 6), dim), (parts,), jnp.float32, low / len(pieces), high / len(pieces))
        return jnp.repeat(jnp.exp(steps), dims[dim] // parts).reshape((-1,) + (1,) * (len(dims) - dim - 1))

    loudness = one(*pieces[0])
    for cut in pieces[1:]:
        loudness = loudness * one(*cut)
    return loudness


def gaussian(key, shape, spread, reach, cuts=(), held_as=jnp.bfloat16):
    drawn = spread * jax.random.normal(key, shape, jnp.float32)
    if cuts:
        drawn = drawn * shard_levels(key, shape, cuts, -0.22, 0.18)
    return jnp.clip(drawn, -reach, reach).astype(held_as)


def setup_inputs(seed: int = 0) -> dict:
    keys = jax.random.split(jax.random.key(seed), 7)
    front = draw_front(jax.random.fold_in(keys[6], 71), 0)
    bases = draw_bases(jax.random.fold_in(keys[6], 71), 0)
    ranks = with_ends(jax.random.randint(keys[2], (NBLK, NP), RLO, RMAX + 1), jax.random.fold_in(keys[2], 1), RLO, RMAX).astype(jnp.int32)
    child_map = draw_child_map(jax.random.fold_in(keys[6], 71), 0)
    child_factors = gaussian(keys[4], (CHILDREN, NC, RC), 0.35, 2.1, ((0, 4), (1, 64)), jnp.float32)
    child_weights = jnp.clip(jnp.exp(jax.random.uniform(keys[5], (CHILDREN, RC), jnp.float32, math.log(0.1), math.log(1.0))), 0.1, 1.0)
    return {"front": front, "bases": bases, "ranks": ranks, "child_map": child_map, "child_factors": child_factors, "child_weights": child_weights}


highest = lax.Precision.HIGHEST

def reference(front, bases, ranks, child_map, child_factors, child_weights):
    matrix = front
    inside = jnp.arange(BS, dtype=jnp.int32)
    for child_index in range(CHILDREN):
        scaled = child_factors[child_index] * child_weights[child_index][None, :]
        contrib = jnp.dot(scaled.astype(jnp.float32), child_factors[child_index].T.astype(jnp.float32), precision=highest, preferred_element_type=jnp.float32)
        places = (child_map[child_index][:, None] * BS + inside[None, :]).reshape(-1).astype(jnp.int32)
        matrix = matrix.at[places[:, None], places[None, :]].add(contrib)
    rows_all = jnp.arange(NF, dtype=jnp.int32)
    factor_parts = []
    pivot_parts = []
    for pivot_step in range(NP):
        first = pivot_step * BS
        lower = jnp.linalg.cholesky(matrix[first:first + BS, first:first + BS])
        pivot_parts.append(jnp.diagonal(lower) ** 2)
        solved = lax.linalg.triangular_solve(lower, matrix[:, first:first + BS], left_side=False, lower=True, transpose_a=True)
        solved = jnp.where((rows_all >= first + BS)[:, None], solved, jnp.float32(0.0))
        keep = (jnp.arange(RMAX, dtype=jnp.int32)[None, :] < ranks[:, pivot_step][:, None]).astype(jnp.float32)
        basis = bases[:, pivot_step * RMAX:(pivot_step + 1) * RMAX].reshape(NBLK, BS, RMAX) * keep[:, None, :]
        packed = jnp.einsum('bij,bjr->bir', solved.reshape(NBLK, BS, BS), basis, precision=highest)
        expanded = jnp.einsum('bir,bjr->bij', packed, basis, precision=highest).reshape(NF, BS)
        matrix = matrix - jnp.dot(expanded.astype(jnp.float32), expanded.T.astype(jnp.float32), precision=highest, preferred_element_type=jnp.float32)
        factor_parts.append(packed.reshape(NF, RMAX))
    return (matrix, jnp.concatenate(factor_parts, axis=1), jnp.concatenate(pivot_parts))
```

```python
import functools

import jax
import jax.numpy as jnp
from jax import lax
from jax.experimental import pallas as pl
from jax.experimental.pallas import tpu as pltpu
from jax.sharding import PartitionSpec as P

BS = 128
NP = 4
RMAX = 32
LEAD = NP * BS
XR = 40
MESH = pl.DeviceIdType.MESH
F32 = jnp.float32
BF16 = jnp.bfloat16
HI = lax.Precision.HIGHEST
VMEM_LIMIT = 56 * 1024 * 1024


def dot6(a, b, ca, cb):
    return lax.dot_general(
        a, b, (((ca,), (cb,)), ((), ())), precision=HI, preferred_element_type=F32
    )


def split(a):
    high = a.astype(BF16)
    return high, (a - high.astype(F32)).astype(BF16)


def dot3(a, b, ca, cb):
    one = lambda p, q: lax.dot_general(
        p, q, (((ca,), (cb,)), ((), ())), preferred_element_type=F32
    )
    return one(a[0], b[0]) + (one(a[0], b[1]) + one(a[1], b[0]))


def inverse_factor(block, nb=16):
    n = BS
    lane = lax.broadcasted_iota(jnp.int32, (1, n), 1)
    row = lax.broadcasted_iota(jnp.int32, (nb, 1), 0)
    unit = lax.broadcasted_iota(jnp.int32, (n, n), 0) == lax.broadcasted_iota(
        jnp.int32, (n, n), 1
    )
    state = jnp.concatenate([block, unit.astype(F32)], axis=1)
    done = []
    pivots = jnp.zeros((1, n), F32)
    for start in range(0, n, nb):
        head = state[:nb]
        forward = head[:, n:]
        columns = [
            jnp.broadcast_to(head[:, start + j : start + j + 1], (nb, n)) for j in range(nb)
        ]
        scale = jnp.zeros((nb, n), F32)
        for j in range(nb):
            pivot = columns[j][j : j + 1]
            inverse = 1.0 / pivot
            ratio = columns[j] * inverse
            below = jnp.where(row > j, ratio, 0.0)
            other = jnp.where(row == j, 0.0, ratio)
            forward = forward - below * forward[j : j + 1]
            head = head - jnp.concatenate([other, other], axis=1) * head[j : j + 1]
            for i in range(j + 1, nb):
                columns[i] = columns[i] - other * columns[i][j : j + 1]
            scale = jnp.where(row == j, inverse, scale)
            pivots = jnp.where(lane == start + j, pivot, pivots)
        done.append(forward * lax.sqrt(scale))
        if start + nb < n:
            solved = head * jnp.concatenate([scale, scale], axis=1)
            pieces = [solved, jnp.zeros((n - start - nb, 2 * n), F32)]
            if start:
                pieces = [jnp.zeros((start, 2 * n), F32)] + pieces
            rest = state[nb:]
            state = rest - dot6(rest[:, :n], jnp.concatenate(pieces, axis=0), 1, 0)
    return jnp.concatenate(done, axis=0), pivots


def remote(src, dst, send, recv, z, c, y):
    return pltpu.make_async_remote_copy(
        src_ref=src,
        dst_ref=dst,
        send_sem=send,
        recv_sem=recv,
        device_id=(z, c, y),
        device_id_type=MESH,
    )


def here():
    return lax.axis_index("row"), lax.axis_index("col"), lax.axis_index("sub")


def gather_kernel(
    factors, front, bases, every, lead, facing,
    z_send, z_recv, m_send, m_recv, p_send, p_recv, h_send, h_recv,
    l_send, l_recv, g_send, g_recv, s_send, s_recv, local,
):
    z, c, y = here()
    x = c // 2
    core = c % 2
    other = 2 * x + (1 - core)
    place = x * 4 + y

    def column(step):
        return 2 * ((x + step) % 4) + core

    barrier = pltpu.get_barrier_semaphore()

    def greet(step, carry):
        spot = (place + step) % 16
        pl.semaphore_signal(
            barrier, inc=1, device_id=(z, 2 * (spot // 4) + core, spot % 4), device_id_type=MESH
        )
        return carry

    lax.fori_loop(1, 16, greet, 0)
    for step in range(1, 8):
        pl.semaphore_signal(
            barrier, inc=1, device_id=((z + step) % 8, c, y), device_id_type=MESH
        )
    pl.semaphore_signal(barrier, inc=1, device_id=(z, other, y), device_id_type=MESH)
    pl.semaphore_wait(barrier, 23)

    along_z = []
    for step in range(1, 8):
        copy = remote(
            factors.at[0], every.at[y, z, x, core], z_send.at[step], z_recv.at[step],
            (z + step) % 8, c, y,
        )
        copy.start()
        along_z.append(copy)
    own = pltpu.make_async_copy(factors.at[0], every.at[y, z, x, core], local.at[0])
    own.start()

    first = z == 0
    root0 = jnp.logical_and(first, jnp.logical_and(c == 0, y == 0))
    root1 = jnp.logical_and(first, jnp.logical_and(c == 0, y == 1))
    working = jnp.logical_and(first, core == 0)

    def scatter0(spot):
        rows = pl.ds(32 * spot, 32)
        return remote(
            front.at[rows], lead.at[rows, pl.ds(0, 384)], l_send.at[0, spot], l_recv.at[0],
            0, 2 * (spot // 4), spot % 4,
        )

    def scatter1(spot):
        rows = pl.ds(32 * spot, 32)
        return remote(
            front.at[rows, pl.ds(0, 128)], lead.at[rows, pl.ds(384, 128)], l_send.at[1, spot],
            l_recv.at[1], 0, 2 * (spot // 4), spot % 4,
        )

    @pl.when(root0)
    def _():
        for spot in range(1, 16):
            scatter0(spot).start()
        mine = pltpu.make_async_copy(
            front.at[pl.ds(0, 32)], lead.at[pl.ds(0, 32), pl.ds(0, 384)], local.at[1]
        )
        mine.start()
        mine.wait()

    @pl.when(root1)
    def _():
        for spot in range(16):
            if spot != 1:
                scatter1(spot).start()
        mine = pltpu.make_async_copy(
            front.at[pl.ds(32, 32), pl.ds(0, 128)],
            lead.at[pl.ds(32, 32), pl.ds(384, 128)], local.at[1],
        )
        mine.start()
        mine.wait()

    def facing_copy(step):
        return remote(
            bases.at[pl.ds(384 * y, 384)], facing, m_send.at[step], m_recv.at[0],
            (z + step) % 8, c, y,
        )

    @pl.when(z == c)
    def _():
        for step in range(1, 8):
            facing_copy(step).start()
        mine = pltpu.make_async_copy(bases.at[pl.ds(384 * y, 384)], facing, local.at[2])
        mine.start()
        mine.wait()

    my_rows = pl.ds(32 * place, 32)

    def spread(step):
        spot = (place + step) % 16
        return remote(
            lead.at[my_rows], lead.at[my_rows], g_send.at[step], g_recv.at[step],
            0, 2 * (spot // 4), spot % 4,
        )

    @pl.when(working)
    def _():
        @pl.when(place != 0)
        def _():
            scatter0(place).wait_recv()

        @pl.when(place != 1)
        def _():
            scatter1(place).wait_recv()

        for step in range(1, 16):
            spread(step).start()

    low, high = pl.ds(0, 32), pl.ds(32, 32)
    siblings = []

    def sibling(ref):
        number = len(siblings)
        copy = remote(ref, ref, s_send.at[number], s_recv.at[number], z, other, y)
        copy.start()
        siblings.append(copy)

    own.wait()
    for copy in along_z:
        copy.wait_recv()
    second = []
    for step in range(1, 4):
        piece = every.at[y, :, x, core, low]
        copy = remote(
            piece, piece, p_send.at[0, step], p_recv.at[0, step], z, column(step), y
        )
        copy.start()
        piece = every.at[y, :, x, core, high]
        back = remote(
            piece, piece, p_send.at[1, step], p_recv.at[1, step], z, c, (y + step) % 4
        )
        back.start()
        second.append((copy, back))
    sibling(every.at[y, :, x, core])

    @pl.when(working)
    def _():
        for step in range(1, 16):
            spread(step).wait_recv()

    def lead_sibling():
        return remote(lead, lead, g_send.at[0], g_recv.at[0], z, other, y)

    @pl.when(working)
    def _():
        lead_sibling().start()

    for copy, back in second:
        copy.wait_recv()
        back.wait_recv()
    third = []
    for step in range(1, 4):
        piece = every.at[y, :, :, core, low]
        copy = remote(
            piece, piece, h_send.at[0, step], h_recv.at[0, step], z, c, (y + step) % 4
        )
        copy.start()
        piece = every.at[:, :, x, core, high]
        back = remote(
            piece, piece, h_send.at[1, step], h_recv.at[1, step], z, column(step), y
        )
        back.start()
        third.append((copy, back))
    for step in range(1, 4):
        sibling(every.at[y, :, (x + 4 - step) % 4, core, low])
        sibling(every.at[(y + 4 - step) % 4, :, x, core, high])
    for step in range(1, 4):
        copy, back = third[step - 1]
        copy.wait_recv()
        sibling(every.at[(y + 4 - step) % 4, :, :, core, low])
        back.wait_recv()
        sibling(every.at[:, :, (x + 4 - step) % 4, core, high])
    for copy in siblings:
        copy.wait_recv()

    @pl.when(jnp.logical_and(first, core == 1))
    def _():
        lead_sibling().wait_recv()

    @pl.when(z != c)
    def _():
        facing_copy(1).wait_recv()

    for copy in along_z + siblings:
        copy.wait_send()
    for copy, back in second + third:
        copy.wait_send()
        back.wait_send()

    @pl.when(root0)
    def _():
        for spot in range(1, 16):
            scatter0(spot).wait_send()

    @pl.when(root1)
    def _():
        for spot in range(16):
            if spot != 1:
                scatter1(spot).wait_send()

    @pl.when(z == c)
    def _():
        for step in range(1, 8):
            facing_copy(step).wait_send()

    @pl.when(working)
    def _():
        for step in range(1, 16):
            spread(step).wait_send()
        lead_sibling().wait_send()


def gather(factors, front, bases):
    dma = pltpu.SemaphoreType.DMA
    any_space = pl.BlockSpec(memory_space=pl.ANY)
    return pl.pallas_call(
        gather_kernel,
        out_shape=(
            jax.ShapeDtypeStruct((4, 8, 4, 2, 64, BS), F32),
            jax.ShapeDtypeStruct((LEAD, LEAD), F32),
            jax.ShapeDtypeStruct((384, BS), F32),
        ),
        in_specs=[any_space] * 3,
        out_specs=(any_space,) * 3,
        scratch_shapes=[
            dma((8,)), dma((8,)), dma((8,)), dma((1,)), dma((2, 4)), dma((2, 4)),
            dma((2, 4)), dma((2, 4)), dma((2, 16)), dma((2,)), dma((16,)), dma((16,)),
            dma((16,)), dma((16,)), dma((3,)),
        ],
        compiler_params=pltpu.CompilerParams(collective_id=0, has_side_effects=True),
        name="gather",
    )(factors, front, bases)


def rank_mask(ranks, block):
    lane = lax.broadcasted_iota(jnp.int32, (1, BS), 1)
    limit = jnp.zeros((1, BS), jnp.int32)
    for step in range(NP):
        limit = jnp.where(lane // RMAX == step, ranks[block, step], limit)
    return (lane % RMAX < limit).astype(F32)


def assemble_kernel(
    inverse, ranks, every, lead, front, weights, bases, facing, panel, masks, rows, sems
):
    _, c, y = here()
    first_own = (c * 4 + y) * 3
    ids = [0, 1, 2, 3] + [first_own + j for j in range(3)]

    def fetch(child, spot):
        found = jnp.maximum(inverse[child, ids[spot]], 0)
        return pltpu.make_async_copy(
            every.at[child, pl.ds(pl.multiple_of(found * BS, BS), BS)],
            rows.at[child, pl.ds(spot * BS, BS)], sems.at[child, spot],
        )

    for child in range(4):
        for spot in range(7):
            fetch(child, spot).start()
    for spot in range(4):
        masks[spot] = bases[spot * BS : (spot + 1) * BS] * rank_mask(ranks, spot)
    for j in range(3):
        masks[4 + j] = facing[j * BS : (j + 1) * BS] * rank_mask(ranks, first_own + j)
    total = jnp.concatenate(
        [lead[...]] + [front[:, j * BS : (j + 1) * BS].T for j in range(3)], axis=0
    )
    for child in range(4):
        for spot in range(7):
            fetch(child, spot).wait()
        present = jnp.concatenate(
            [
                jnp.full((BS, 1), (inverse[child, ids[spot]] >= 0).astype(F32))
                for spot in range(7)
            ],
            axis=0,
        )
        both = rows[child] * present
        total = total + dot6(both * weights[child : child + 1], both[:LEAD], 1, 1)
    panel[...] = total


def assemble(inverse, ranks, every, lead, front, weights, bases, facing):
    smem = pl.BlockSpec(memory_space=pltpu.SMEM)
    vmem = pl.BlockSpec(memory_space=pltpu.VMEM)
    return pl.pallas_call(
        assemble_kernel,
        grid=(1,),
        out_shape=(
            jax.ShapeDtypeStruct((7 * BS, LEAD), F32),
            jax.ShapeDtypeStruct((7, BS, BS), F32),
        ),
        in_specs=[
            smem, smem, pl.BlockSpec(memory_space=pl.ANY), vmem,
            pl.BlockSpec((LEAD, 384), lambda i: (0, 0)), vmem,
            pl.BlockSpec((LEAD, BS), lambda i: (0, 0)), vmem,
        ],
        out_specs=(vmem, vmem),
        scratch_shapes=[pltpu.VMEM((4, 7 * BS, BS), F32), pltpu.SemaphoreType.DMA((4, 7))],
        compiler_params=pltpu.CompilerParams(vmem_limit_bytes=VMEM_LIMIT),
        name="assemble",
    )(inverse, ranks, every, lead, front, weights, bases, facing)


def chain_kernel(panel, masks, col_out, row_out, work, z_send, z_recv, p_send, p_recv, local):
    z, c, y = here()
    place = c * 4 + y
    barrier = pltpu.get_barrier_semaphore()

    def greet(step, carry):
        spot = (place + step) % 32
        pl.semaphore_signal(
            barrier, inc=1, device_id=(z, spot // 4, spot % 4), device_id_type=MESH
        )
        return carry

    lax.fori_loop(1, 32, greet, 0)
    for step in range(1, 8):
        pl.semaphore_signal(
            barrier, inc=1, device_id=((z + step) % 8, c, y), device_id_type=MESH
        )
    pl.semaphore_wait(barrier, 38)

    def down(t, k):
        target = (c + k) % 8
        return target, remote(
            col_out.at[t], col_out.at[t], z_send.at[t, k], z_recv.at[t], target, c, y
        )

    def across(t, step):
        spot = (place + step) % 32
        return remote(
            col_out.at[t], row_out.at[t, y], p_send.at[t, step], p_recv.at[t, y],
            z, spot // 4, spot % 4,
        )

    def own(t):
        return pltpu.make_async_copy(col_out.at[t], row_out.at[t, y], local.at[t])

    def share(t):
        @pl.when(z == c)
        def _():
            lax.fori_loop(1, 32, lambda s, k: (across(t, s).start(), k)[1], 0)
            own(t).start()

    @pl.when(z == 0)
    def _():
        work[...] = panel[...]
        for t in range(NP):
            cols = slice(t * BS, (t + 1) * BS)
            ranks = slice(t * RMAX, (t + 1) * RMAX)
            inverse, pivots = inverse_factor(work[t * BS : (t + 1) * BS, cols])
            heads = {}
            for i in range(t + 1, NP):
                solved = dot6(work[i * BS : (i + 1) * BS, cols], inverse, 1, 1)
                basis = masks[i][:, ranks]
                packed = dot6(solved, basis, 1, 0)
                heads[i] = dot6(packed, basis, 1, 1)
                for later in range(t + 1, i + 1):
                    spot = (slice(i * BS, (i + 1) * BS), slice(later * BS, (later + 1) * BS))
                    work[spot] = work[spot] - dot6(heads[i], heads[later], 1, 1)
            for j in range(3):
                own_rows = slice((4 + j) * BS, (5 + j) * BS)
                solved = dot6(work[own_rows, cols], inverse, 1, 1)
                solved = jnp.where(place * 3 + j > t, solved, 0.0)
                basis = masks[4 + j][:, ranks]
                packed = dot6(basis, solved, 0, 1)
                col_out[t, :RMAX, j * BS : (j + 1) * BS] = packed
                col_out[t, RMAX:, j * BS : (j + 1) * BS] = jnp.broadcast_to(pivots, (8, BS))
                if t + 1 < NP:
                    head = dot6(packed, basis, 0, 1)
                    for later in range(t + 1, NP):
                        spot = (own_rows, slice(later * BS, (later + 1) * BS))
                        work[spot] = work[spot] - dot6(head, heads[later], 1, 1)
            for k in range(8):
                target, copy = down(t, k)

                @pl.when(target != 0)
                def _():
                    copy.start()

            share(t)

    @pl.when(z != 0)
    def _():
        for t in range(NP):
            down(t, 0)[1].wait_recv()
            share(t)

    for t in range(NP):
        for step in range(4):
            @pl.when(jnp.logical_or(z != c, y != step))
            def _():
                remote(
                    col_out.at[t], row_out.at[t, step], p_send.at[t, 1], p_recv.at[t, step],
                    z, c, y,
                ).wait_recv()

    @pl.when(z == 0)
    def _():
        for t in range(NP):
            for k in range(8):
                target, copy = down(t, k)

                @pl.when(target != 0)
                def _():
                    copy.wait_send()

    @pl.when(z == c)
    def _():
        for t in range(NP):
            lax.fori_loop(1, 32, lambda s, k: (across(t, s).wait_send(), k)[1], 0)
            own(t).wait()


def chain(panel, masks):
    dma = pltpu.SemaphoreType.DMA
    vmem = pl.BlockSpec(memory_space=pltpu.VMEM)
    return pl.pallas_call(
        chain_kernel,
        out_shape=(
            jax.ShapeDtypeStruct((NP, XR, 384), F32),
            jax.ShapeDtypeStruct((NP, 4, XR, 384), F32),
        ),
        in_specs=[vmem, vmem],
        out_specs=(vmem, vmem),
        scratch_shapes=[
            pltpu.VMEM((7 * BS, LEAD), F32),
            dma((NP, 8)), dma((NP,)), dma((NP, 32)), dma((NP, 4)), dma((NP,)),
        ],
        compiler_params=pltpu.CompilerParams(
            collective_id=1, has_side_effects=True, vmem_limit_bytes=VMEM_LIMIT
        ),
        name="chain",
    )(panel, masks)


def update_kernel(
    inverse, every, front, weights, bases, facing, col_x, row_x, out, factors, pivots,
    row_side, col_side, col_split, heads, row_sems, col_sems,
):
    z, c, y = here()
    i = pl.program_id(0)
    groups = 12
    first_col = (c * 4 + y) * 3

    def row_copy(child, group):
        found = inverse[child, z * groups + group]
        return found, pltpu.make_async_copy(
            every.at[child, pl.ds(pl.multiple_of(jnp.maximum(found, 0) * BS, BS), BS)],
            row_side.at[group, child], row_sems.at[group, child],
        )

    def col_copy(child, j):
        found = inverse[child, first_col + j]
        return found, pltpu.make_async_copy(
            every.at[child, pl.ds(pl.multiple_of(jnp.maximum(found, 0) * BS, BS), BS)],
            col_side.at[child, pl.ds(j * BS, BS)], col_sems.at[child, j],
        )

    @pl.when(i == 0)
    def _():
        for child in range(4):
            for j in range(3):
                found, copy = col_copy(child, j)

                @pl.when(found >= 0)
                def _():
                    copy.start()

                @pl.when(found < 0)
                def _():
                    col_side[child, j * BS : (j + 1) * BS] = jnp.zeros((BS, BS), F32)

        def begin(group, carry):
            for child in range(4):
                found, copy = row_copy(child, group)

                @pl.when(found >= 0)
                def _():
                    copy.start()

            return carry

        lax.fori_loop(0, groups, begin, 0)
        for t in range(NP):
            ranks = slice(t * RMAX, (t + 1) * RMAX)
            for j in range(3):
                cols = slice(j * BS, (j + 1) * BS)
                head = dot6(facing[cols, ranks], col_x[t, :RMAX, cols], 1, 0)
                high, low = split(head)
                heads[0, t, :, cols] = high
                heads[1, t, :, cols] = low
            pivots[t : t + 1, :] = col_x[t, RMAX : RMAX + 1, :BS]
        for child in range(4):
            for j in range(3):
                found, copy = col_copy(child, j)

                @pl.when(found >= 0)
                def _():
                    copy.wait()

            high, low = split(col_side[child])
            col_split[0, child] = high
            col_split[1, child] = low

    total = front[...]
    quarter = i // 3
    start = pl.multiple_of((i % 3) * BS, BS)
    packed = jnp.concatenate(
        [row_x[t, quarter, :RMAX, pl.ds(start, BS)] for t in range(NP)], axis=0
    ).T
    factors[...] = packed
    turned = split(bases[...].T)
    inner = jnp.concatenate(
        [
            dot3(
                tuple(part[t * RMAX : (t + 1) * RMAX] for part in turned),
                (heads[0, t], heads[1, t]), 1, 0,
            )
            for t in range(NP)
        ],
        axis=0,
    )
    out[...] = total - dot3(split(packed), split(inner), 1, 0)
    for child in range(4):
        found, copy = row_copy(child, i)

        @pl.when(found >= 0)
        def _():
            copy.wait()
            scaled = split(row_side[i, child] * weights[child : child + 1])
            out[...] += dot3(scaled, (col_split[0, child], col_split[1, child]), 1, 1)


def update(inverse, every, front, weights, bases, facing, col_x, row_x):
    smem = pl.BlockSpec(memory_space=pltpu.SMEM)
    vmem = pl.BlockSpec(memory_space=pltpu.VMEM)
    return pl.pallas_call(
        update_kernel,
        grid=(12,),
        out_shape=(
            jax.ShapeDtypeStruct((1536, 384), F32),
            jax.ShapeDtypeStruct((1536, BS), F32),
            jax.ShapeDtypeStruct((NP, BS), F32),
        ),
        in_specs=[
            smem, pl.BlockSpec(memory_space=pl.ANY),
            pl.BlockSpec((BS, 384), lambda i: (i, 0)), vmem,
            pl.BlockSpec((BS, BS), lambda i: (i, 0)), vmem, vmem, vmem,
        ],
        out_specs=(
            pl.BlockSpec((BS, 384), lambda i: (i, 0)),
            pl.BlockSpec((BS, BS), lambda i: (i, 0)),
            pl.BlockSpec((NP, BS), lambda i: (0, 0)),
        ),
        scratch_shapes=[
            pltpu.VMEM((12, 4, BS, BS), F32),
            pltpu.VMEM((4, 384, BS), F32),
            pltpu.VMEM((2, 4, 384, BS), BF16),
            pltpu.VMEM((2, NP, BS, 384), BF16),
            pltpu.SemaphoreType.DMA((12, 4)),
            pltpu.SemaphoreType.DMA((4, 3)),
        ],
        compiler_params=pltpu.CompilerParams(vmem_limit_bytes=VMEM_LIMIT),
        name="update",
    )(inverse, every, front, weights, bases, facing, col_x, row_x)


def body(front, bases, ranks, child_map, child_factors, child_weights):
    blocks = ranks.shape[0]
    hit = child_map[:, None, :] == jnp.arange(blocks, dtype=jnp.int32)[None, :, None]
    order = jnp.arange(1, child_map.shape[1] + 1, dtype=jnp.int32)
    inverse = jnp.max(jnp.where(hit, order, 0), axis=2) - 1
    every, lead, facing = gather(child_factors, front, bases)
    every = every.reshape(4, 4096, BS)
    panel, masks = assemble(inverse, ranks, every, lead, front, child_weights, bases, facing)
    col_x, row_x = chain(panel, masks)
    out, factors, pivots = update(
        inverse, every, front, child_weights, bases, facing, col_x, row_x
    )
    return out, factors, pivots.reshape(NP * BS)


def solution(mesh):
    in_specs = (
        P("row", ("col", "sub")),
        P("row", None),
        P(),
        P(),
        P("sub", ("row", "col"), None),
        P(),
    )
    out_specs = (P("row", ("col", "sub")), P("row", None), P())
    return jax.shard_map(body, mesh=mesh, in_specs=in_specs, out_specs=out_specs, check_vma=False)
```

```python
import functools

import jax
import jax.numpy as jnp
from jax import lax
from jax.experimental import pallas as pl
from jax.experimental.pallas import tpu as pltpu
from jax.sharding import PartitionSpec as P

BS = 128
NP = 4
RMAX = 32
LEAD = NP * BS
XR = 40
MESH = pl.DeviceIdType.MESH
F32 = jnp.float32
BF16 = jnp.bfloat16
HI = lax.Precision.HIGHEST
VMEM_LIMIT = 56 * 1024 * 1024


def dot6(a, b, ca, cb):
    return lax.dot_general(
        a, b, (((ca,), (cb,)), ((), ())), precision=HI, preferred_element_type=F32
    )


def split(a):
    high = a.astype(BF16)
    return high, (a - high.astype(F32)).astype(BF16)


def dot3(a, b, ca, cb):
    one = lambda p, q: lax.dot_general(
        p, q, (((ca,), (cb,)), ((), ())), preferred_element_type=F32
    )
    return one(a[0], b[0]) + (one(a[0], b[1]) + one(a[1], b[0]))


def inverse_factor(block, nb=16):
    n = BS
    lane = lax.broadcasted_iota(jnp.int32, (1, n), 1)
    row = lax.broadcasted_iota(jnp.int32, (nb, 1), 0)
    unit = lax.broadcasted_iota(jnp.int32, (n, n), 0) == lax.broadcasted_iota(
        jnp.int32, (n, n), 1
    )
    state = jnp.concatenate([block, unit.astype(F32)], axis=1)
    done = []
    pivots = jnp.zeros((1, n), F32)
    for start in range(0, n, nb):
        head = state[:nb]
        forward = head[:, n:]
        columns = [
            jnp.broadcast_to(head[:, start + j : start + j + 1], (nb, n)) for j in range(nb)
        ]
        scale = jnp.zeros((nb, n), F32)
        for j in range(nb):
            pivot = columns[j][j : j + 1]
            inverse = 1.0 / pivot
            ratio = columns[j] * inverse
            below = jnp.where(row > j, ratio, 0.0)
            other = jnp.where(row == j, 0.0, ratio)
            forward = forward - below * forward[j : j + 1]
            head = head - jnp.concatenate([other, other], axis=1) * head[j : j + 1]
            for i in range(j + 1, nb):
                columns[i] = columns[i] - other * columns[i][j : j + 1]
            scale = jnp.where(row == j, inverse, scale)
            pivots = jnp.where(lane == start + j, pivot, pivots)
        done.append(forward * lax.sqrt(scale))
        if start + nb < n:
            solved = head * jnp.concatenate([scale, scale], axis=1)
            pieces = [solved, jnp.zeros((n - start - nb, 2 * n), F32)]
            if start:
                pieces = [jnp.zeros((start, 2 * n), F32)] + pieces
            rest = state[nb:]
            state = rest - dot6(rest[:, :n], jnp.concatenate(pieces, axis=0), 1, 0)
    return jnp.concatenate(done, axis=0), pivots


def remote(src, dst, send, recv, z, c, y):
    return pltpu.make_async_remote_copy(
        src_ref=src,
        dst_ref=dst,
        send_sem=send,
        recv_sem=recv,
        device_id=(z, c, y),
        device_id_type=MESH,
    )


def here():
    return lax.axis_index("row"), lax.axis_index("col"), lax.axis_index("sub")


LOWER = [(0, 0), (1, 0), (2, 0), (3, 0), (1, 1), (2, 1), (3, 1), (2, 2), (3, 2), (3, 3)]
PIECE = 80
LOW = 32


def fragments(spot):
    found = []
    row = spot * PIECE
    while row < (spot + 1) * PIECE:
        block, inside = divmod(row, BS)
        rows = min(BS - inside, (spot + 1) * PIECE - row)
        found.append((len(found), row, rows, block, inside))
        row += rows
    return found


def blk(i):
    return slice(i * BS, (i + 1) * BS)


def rank_limit(ranks, block):
    lane = lax.broadcasted_iota(jnp.int32, (1, BS), 1)
    found = ranks[pl.ds(block, 1), :]
    limit = jnp.zeros((1, BS), jnp.int32)
    for t in range(NP):
        limit = jnp.where(lane // RMAX == t, found[:, t : t + 1], limit)
    return (lane % RMAX < limit).astype(F32)


def sweep_kernel(
    inverse, ranks, weights, factors, front, bases,
    every, facing, col_out, row_out,
    ez, ex, cand, wx, wl, lead, staged, wc, fpan, blead,
    z_send, z_recv, m_send, m_recv, l_send, l_recv, g_send, g_recv, w_send, w_recv,
    v_send, v_recv, b_send, b_recv, a_send, a_recv, r_send, r_recv, t_send, t_recv,
    u_send, u_recv, k_send, k_recv, s_send, s_recv, d_send, d_recv, p_send, p_recv,
    q_send, q_recv, local,
):
    z, c, y = here()
    x = c // 2
    core = c % 2
    other = 2 * x + (1 - core)
    spot16 = x * 4 + y
    place = c * 4 + y
    first = z == 0
    root0 = jnp.logical_and(first, place == 0)
    root1 = jnp.logical_and(first, place == 1)
    working = jnp.logical_and(first, core == 0)
    low, high = pl.ds(0, LOW), pl.ds(LOW, 64 - LOW)

    def column(step):
        return 2 * ((x + step) % 4) + core

    def xs(step):
        return (x + step) % 4

    def ys(step):
        return (y + step) % 4

    own_ez = pltpu.make_async_copy(factors.at[0], ez.at[z], local.at[0])
    own_front = pltpu.make_async_copy(front.at[pl.ds(0, LEAD)], fpan, local.at[1])
    own_bases = pltpu.make_async_copy(bases.at[pl.ds(0, LEAD)], blead, local.at[2])
    own_ex = pltpu.make_async_copy(ez, ex.at[:, x], local.at[3])
    own_every = pltpu.make_async_copy(ex, every.at[y, :, :, core], local.at[4])
    own_facing = pltpu.make_async_copy(bases.at[pl.ds(384 * y, 384)], facing, local.at[5])
    own_ez.start()

    @pl.when(first)
    def _():
        own_front.start()
        own_bases.start()

    @pl.when(z == c)
    def _():
        own_facing.start()

    barrier = pltpu.get_barrier_semaphore()

    def greet(step, carry):
        spot = (place + step) % 32
        pl.semaphore_signal(
            barrier, inc=1, device_id=(z, spot // 4, spot % 4), device_id_type=MESH
        )
        return carry

    lax.fori_loop(1, 32, greet, 0)
    for step in range(1, 8):
        pl.semaphore_signal(
            barrier, inc=1, device_id=((z + step) % 8, c, y), device_id_type=MESH
        )
    pl.semaphore_wait(barrier, 38)

    def along_z(target):
        return remote(factors.at[0], ez.at[z], z_send.at[target], z_recv.at[z], target, c, y)

    def along_z_from(source):
        return remote(
            factors.at[0], ez.at[source], z_send.at[source], z_recv.at[source], source, c, y
        )

    @pl.when(z != 0)
    def _():
        along_z(0).start()

    def scatter(spot, part):
        number, row, rows, block, inside = part
        i, k = LOWER[block]
        return remote(
            front.at[pl.ds(i * BS + inside, rows), pl.ds((k % 3) * BS, BS)],
            lead.at[pl.ds(row, rows)], l_send.at[spot, number], l_recv.at[number],
            0, 2 * (spot // 4), spot % 4,
        )

    def scatters(root):
        for spot in range(16):
            for part in fragments(spot):
                if (part[3] == 9) == (root == 1) and spot != root:
                    yield spot, part

    @pl.when(root0)
    def _():
        for spot, part in scatters(0):
            scatter(spot, part).start()
        mine = pltpu.make_async_copy(
            front.at[pl.ds(0, PIECE), pl.ds(0, BS)], lead.at[pl.ds(0, PIECE)], local.at[6]
        )
        mine.start()
        mine.wait()

    @pl.when(root1)
    def _():
        for spot, part in scatters(1):
            scatter(spot, part).start()

    for step in range(1, 8):
        target = (z + step) % 8

        @pl.when(target != 0)
        def _():
            along_z(target).start()

    def facing_copy(step):
        return remote(
            bases.at[pl.ds(384 * y, 384)], facing, m_send.at[step], m_recv.at[0],
            (z + step) % 8, c, y,
        )

    @pl.when(z == c)
    def _():
        for step in range(1, 8):
            facing_copy(step).start()

    my_rows = pl.ds(pl.multiple_of(PIECE * spot16, 8), PIECE)

    def spread(step):
        spot = (spot16 + step) % 16
        return remote(
            lead.at[my_rows], lead.at[my_rows], g_send.at[step], g_recv.at[step],
            0, 2 * (spot // 4), spot % 4,
        )

    def spread_from(step):
        spot = (spot16 + 16 - step) % 16
        rows = pl.ds(pl.multiple_of(PIECE * spot, 8), PIECE)
        return remote(
            lead.at[rows], lead.at[rows], g_send.at[step], g_recv.at[step],
            0, 2 * (spot // 4), spot % 4,
        )

    @pl.when(working)
    def _():
        for spot in range(1, 16):
            @pl.when(spot16 == spot)
            def _():
                for part in fragments(spot):
                    scatter(spot, part).wait_recv()

        for step in range(1, 16):
            spread(step).start()

    own_ez.wait()
    for step in range(1, 8):
        along_z_from((z + step) % 8).wait_recv()

    def choose(step):
        return remote(
            cand.at[xs(step)], wx.at[x], w_send.at[step], w_recv.at[step], z, column(step), y
        )

    def choose_from(step):
        return remote(
            cand.at[xs(step)], wx.at[xs(4 - step)], w_send.at[step], w_recv.at[step],
            z, column(step), y,
        )

    def leading(step):
        spot = (spot16 + step) % 16
        return remote(
            wl.at[y, x, core], wl.at[y, x, core], v_send.at[step], v_recv.at[step],
            z, 2 * (spot // 4) + core, spot % 4,
        )

    def leading_from(step):
        spot = (spot16 + 16 - step) % 16
        piece = wl.at[spot % 4, spot // 4, core]
        return remote(
            piece, piece, v_send.at[step], v_recv.at[step],
            z, 2 * (spot // 4) + core, spot % 4,
        )

    @pl.when(first)
    def _():
        for p in range(NP):
            found = inverse[y, p]
            held = jnp.logical_and(found >= 0, found % 4 == x)
            rows = ez[jnp.maximum(found, 0) // 4]
            cand[p] = jnp.where(held, rows, 0.0)
        for step in range(1, 4):
            choose(step).start()
        total = cand[x]
        for step in range(1, 4):
            choose_from(step).wait_recv()
            total = total + wx[xs(4 - step)]
        wl[y, x, core] = total
        for step in range(1, 16):
            leading(step).start()

    def over_x(step):
        return remote(ez, ex.at[:, x], b_send.at[step], b_recv.at[step], z, column(step), y)

    def over_x_from(step):
        return remote(
            ez, ex.at[:, xs(4 - step)], b_send.at[step], b_recv.at[step], z, column(step), y
        )

    def over_y(step):
        return remote(
            ez.at[:, high], every.at[y, :, x, core, high], a_send.at[step], a_recv.at[step],
            z, c, ys(step),
        )

    def over_y_from(step):
        return remote(
            ez.at[:, high], every.at[ys(4 - step), :, x, core, high], a_send.at[step],
            a_recv.at[step], z, c, ys(step),
        )

    own_ex.start()
    for step in range(1, 4):
        over_x(step).start()
        over_y(step).start()

    def then_y(step):
        return remote(
            ex.at[:, :, low], every.at[y, :, :, core, low], r_send.at[step], r_recv.at[step],
            z, c, ys(step),
        )

    def then_y_from(step):
        return remote(
            ex.at[:, :, low], every.at[ys(4 - step), :, :, core, low], r_send.at[step],
            r_recv.at[step], z, c, ys(step),
        )

    def then_x(step, child):
        piece = every.at[ys(child), :, x, core, high]
        return remote(
            piece, piece, t_send.at[step, child], t_recv.at[step, child], z, column(step), y
        )

    def then_x_from(step, child):
        piece = every.at[ys(child), :, xs(4 - step), core, high]
        return remote(
            piece, piece, t_send.at[step, child], t_recv.at[step, child], z, column(step), y
        )

    def to_sibling(number, src, dst):
        return remote(src, dst, s_send.at[number], s_recv.at[number], z, other, y)

    def sibling_ex():
        return to_sibling(0, ex, every.at[y, :, :, core])

    def sibling_a(step):
        piece = every.at[ys(4 - step), :, x, core, high]
        return to_sibling(step, piece, piece)

    def sibling_r(step):
        piece = every.at[ys(4 - step), :, :, core, low]
        return to_sibling(3 + step, piece, piece)

    def sibling_t(step, child):
        piece = every.at[ys(child), :, xs(4 - step), core, high]
        return to_sibling(3 + 3 * step + child, piece, piece)

    def finish_x():
        own_ex.wait()
        for step in range(1, 4):
            over_x_from(step).wait_recv()

    def go_then_y():
        for step in range(1, 4):
            then_y(step).start()
        own_every.start()
        sibling_ex().start()

    def go_then_x():
        for step in range(1, 4):
            over_y_from(step).wait_recv()
        for step in range(1, 4):
            for child in range(1, 4):
                then_x(step, child).start()
        for step in range(1, 4):
            sibling_a(step).start()

    def finish_children():
        for step in range(1, 4):
            then_y_from(step).wait_recv()
            sibling_r(step).start()
            for child in range(1, 4):
                then_x_from(step, child).wait_recv()
                sibling_t(step, child).start()

    def down(t, k):
        target = (c + k) % 8
        return target, remote(
            col_out.at[t], col_out.at[t], d_send.at[t, k], d_recv.at[t], target, c, y
        )

    def across(t, step):
        spot = (spot16 + step) % 16
        return remote(
            col_out.at[t], row_out.at[t, y], p_send.at[t, step], p_recv.at[t, y],
            z, 2 * (spot // 4) + core, spot % 4,
        )

    def own_rows(t):
        return pltpu.make_async_copy(col_out.at[t], row_out.at[t, y], local.at[7 + t])

    def share(t):
        @pl.when(z == c)
        def _():
            own_rows(t).start()
            lax.fori_loop(1, 16, lambda s, k: (across(t, s).start(), k)[1], 0)

    def row_sibling(t, quarter):
        piece = row_out.at[t, quarter]
        return remote(
            piece, piece, q_send.at[t, quarter], q_recv.at[t, quarter], z, other, y
        )

    @pl.when(first)
    def _():
        def pair_lead():
            return remote(lead, lead, k_send.at[0], k_recv.at[0], z, other, y)

        def pair_leading(side):
            piece = wl.at[:, :, side]
            return remote(piece, piece, k_send.at[1], k_recv.at[1], z, other, y)

        @pl.when(core == 0)
        def _():
            for step in range(1, 16):
                spread_from(step).wait_recv()
            pair_lead().start()

        for step in range(1, 16):
            leading_from(step).wait_recv()
        pair_leading(core).start()
        own_bases.wait()
        masks = [blead[blk(i)] * rank_limit(ranks, i) for i in range(NP)]
        projectors = {}
        for i in range(1, NP):
            for t in range(i):
                basis = masks[i][:, t * RMAX : (t + 1) * RMAX]
                projectors[t, i] = dot6(basis, basis, 1, 1)

        @pl.when(core == 1)
        def _():
            pair_lead().wait_recv()

        pair_leading(1 - core).wait_recv()
        plain = jnp.concatenate([wl[s].reshape(LEAD, BS) for s in range(4)], axis=1)
        wide = jnp.concatenate(
            [wl[s].reshape(LEAD, BS) * weights[s : s + 1] for s in range(4)], axis=1
        )
        left = dot6(wide, plain[: 2 * BS], 1, 1)
        right = dot6(wide[2 * BS :], plain[2 * BS :], 1, 1)
        state = {}
        for number, (i, k) in enumerate(LOWER):
            added = left[blk(i), blk(k)] if k < 2 else right[blk(i - 2), blk(k - 2)]
            state[i, k] = lead[blk(number)] + added

        def route(side, step):
            return remote(
                staged.at[2 * step + side], wc.at[y, :, core], u_send.at[side, step],
                u_recv.at[side, step], z, 2 * x + (core + side) % 2, ys(step),
            )

        def route_from(side, step):
            return remote(
                staged.at[2 * step + side], wc.at[ys(4 - step), :, (core + side) % 2],
                u_send.at[side, step], u_recv.at[side, step], z,
                2 * x + (core + side) % 2, ys(step),
            )

        def go_route():
            for step in range(4):
                for side in range(2):
                    target = (2 * x + (core + side) % 2) * 4 + ys(step)
                    for j in range(3):
                        found = inverse[y, target * 3 + j]
                        spot = jnp.maximum(found, 0)
                        rows = ex[spot // 4, spot % 4]
                        rows = jnp.where(found >= 0, rows, 0.0)
                        if side or step:
                            staged[2 * step + side, j] = rows
                        else:
                            wc[y, j, core] = rows
                    if side or step:
                        route(side, step).start()

        panel = {}

        def begin_own():
            for step in range(4):
                for side in range(2):
                    if side or step:
                        route_from(side, step).wait_recv()
            own_front.wait()

            @pl.when(z != c)
            def _():
                facing_copy(1).wait_recv()

            @pl.when(z == c)
            def _():
                own_facing.wait()

            rows = jnp.concatenate(
                [wc[s].reshape(3 * BS, BS) * weights[s : s + 1] for s in range(4)], axis=1
            )
            panel["rows"] = fpan[...].T + dot3(split(rows), split(plain), 1, 1)
            for j in range(3):
                panel[j] = facing[blk(j)] * rank_limit(ranks, place * 3 + j)

        def own_step(t, factor, pivots, heads):
            rows = panel["rows"]
            solved = dot3(split(rows[:, :BS]), split(factor), 1, 1)
            spans = []
            for j in range(3):
                basis = split(panel[j][:, t * RMAX : (t + 1) * RMAX])
                part = jnp.where(place * 3 + j > t, solved[blk(j)], 0.0)
                packed = dot3(basis, split(part), 0, 1)
                col_out[t, :RMAX, blk(j)] = packed
                col_out[t, RMAX:, blk(j)] = jnp.broadcast_to(pivots, (XR - RMAX, BS))
                if t + 1 < NP:
                    spans.append(dot3(split(packed), basis, 0, 1))
            if t + 1 < NP:
                span = split(jnp.concatenate(spans, axis=0))
                later = split(jnp.concatenate([heads[k] for k in range(t + 1, NP)], axis=0))
                panel["rows"] = rows[:, BS:] - dot3(span, later, 1, 1)
            for k in range(8):
                target, copy = down(t, k)

                @pl.when(target != 0)
                def _():
                    copy.start()

            share(t)

        steps = []
        for t in range(NP):
            factor, pivots = inverse_factor(state[t, t])
            heads = {}
            for i in range(t + 1, NP):
                solved = dot6(state[i, t], factor, 1, 1)
                heads[i] = dot6(solved, projectors[t, i], 1, 0)
                for k in range(t + 1, i + 1):
                    state[i, k] = state[i, k] - dot6(heads[i], heads[k], 1, 1)
            steps.append((t, factor, pivots, heads))
            if t == 0:
                finish_x()
                go_route()
                go_then_y()
                go_then_x()
            if t == 2:
                begin_own()
                for done in steps:
                    own_step(*done)
        own_step(*steps[-1])
        finish_children()
        pair_leading(core).wait_send()

        @pl.when(core == 0)
        def _():
            pair_lead().wait_send()

        for step in range(4):
            for side in range(2):
                if side or step:
                    route(side, step).wait_send()

    @pl.when(jnp.logical_not(first))
    def _():
        finish_x()
        go_then_y()
        go_then_x()
        finish_children()

        @pl.when(z != c)
        def _():
            facing_copy(1).wait_recv()

        @pl.when(z == c)
        def _():
            own_facing.wait()

        for t in range(NP):
            down(t, 0)[1].wait_recv()
            share(t)

    holder = z % 2
    for t in range(NP):
        for quarter in range(4):
            @pl.when(core == holder)
            def _():
                mine = jnp.logical_and(z == c, y == quarter)

                @pl.when(mine)
                def _():
                    own_rows(t).wait()

                @pl.when(jnp.logical_not(mine))
                def _():
                    remote(
                        col_out.at[t], row_out.at[t, quarter], p_send.at[t, 1],
                        p_recv.at[t, quarter], z, c, y,
                    ).wait_recv()

                row_sibling(t, quarter).start()

    @pl.when(core != holder)
    def _():
        for t in range(NP):
            for quarter in range(4):
                row_sibling(t, quarter).wait_recv()

    own_every.wait()

    def sibling_all():
        return [sibling_ex()] + [sibling_a(step) for step in range(1, 4)] + [
            sibling_r(step) for step in range(1, 4)
        ] + [sibling_t(step, child) for step in range(1, 4) for child in range(1, 4)]

    for copy in sibling_all():
        copy.wait()
    for step in range(1, 4):
        over_x(step).wait_send()
        over_y(step).wait_send()
        then_y(step).wait_send()
        for child in range(1, 4):
            then_x(step, child).wait_send()
    for step in range(1, 8):
        along_z((z + step) % 8).wait_send()

    @pl.when(first)
    def _():
        for step in range(1, 4):
            choose(step).wait_send()
        for step in range(1, 16):
            leading(step).wait_send()
        for t in range(NP):
            for k in range(8):
                target, copy = down(t, k)

                @pl.when(target != 0)
                def _():
                    copy.wait_send()

    @pl.when(root0)
    def _():
        for spot, part in scatters(0):
            scatter(spot, part).wait_send()

    @pl.when(root1)
    def _():
        for spot, part in scatters(1):
            scatter(spot, part).wait_send()

    @pl.when(working)
    def _():
        for step in range(1, 16):
            spread(step).wait_send()

    @pl.when(z == c)
    def _():
        for step in range(1, 8):
            facing_copy(step).wait_send()
        for t in range(NP):
            lax.fori_loop(1, 16, lambda s, k: (across(t, s).wait_send(), k)[1], 0)

    @pl.when(core == holder)
    def _():
        for t in range(NP):
            for quarter in range(4):
                row_sibling(t, quarter).wait_send()


def sweep(inverse, ranks, weights, factors, front, bases):
    dma = pltpu.SemaphoreType.DMA
    hbm = pl.BlockSpec(memory_space=pl.ANY)
    vmem = pl.BlockSpec(memory_space=pltpu.VMEM)
    half = (64, BS)
    return pl.pallas_call(
        sweep_kernel,
        out_shape=(
            jax.ShapeDtypeStruct((4, 8, 4, 2) + half, F32),
            jax.ShapeDtypeStruct((384, BS), F32),
            jax.ShapeDtypeStruct((NP, XR, 384), F32),
            jax.ShapeDtypeStruct((NP, 4, XR, 384), F32),
        ),
        in_specs=[pl.BlockSpec(memory_space=pltpu.SMEM), vmem, vmem, hbm, hbm, hbm],
        out_specs=(hbm, vmem, vmem, vmem),
        scratch_shapes=[
            pltpu.VMEM((8,) + half, F32),
            pltpu.VMEM((8, 4) + half, F32),
            pltpu.VMEM((4,) + half, F32),
            pltpu.VMEM((4,) + half, F32),
            pltpu.VMEM((4, 4, 2) + half, F32),
            pltpu.VMEM((10 * BS, BS), F32),
            pltpu.VMEM((8, 3) + half, F32),
            pltpu.VMEM((4, 3, 2) + half, F32),
            pltpu.VMEM((LEAD, 384), F32),
            pltpu.VMEM((LEAD, BS), F32),
            dma((8,)), dma((8,)), dma((8,)), dma((1,)), dma((16, 2)), dma((2,)),
            dma((16,)), dma((16,)), dma((4,)), dma((4,)),
            dma((16,)), dma((16,)), dma((4,)), dma((4,)), dma((4,)), dma((4,)),
            dma((4,)), dma((4,)), dma((4, 4)), dma((4, 4)),
            dma((2, 4)), dma((2, 4)), dma((2,)), dma((2,)), dma((16,)), dma((16,)),
            dma((NP, 8)), dma((NP,)), dma((NP, 16)), dma((NP, 4)),
            dma((NP, 4)), dma((NP, 4)), dma((11,)),
        ],
        compiler_params=pltpu.CompilerParams(
            collective_id=0, has_side_effects=True, vmem_limit_bytes=VMEM_LIMIT
        ),
        name="sweep",
    )(inverse, ranks, weights, factors, front, bases)


def update_kernel(
    inverse, every, front, weights, bases, facing, col_x, row_x, out, factors, pivots,
    row_side, col_side, right, row_sems, col_sems,
):
    z, c, y = here()
    q = pl.program_id(0)
    first_col = (c * 4 + y) * 3
    blk = lambda j: slice(j * BS, (j + 1) * BS)

    def row_copy(child, group):
        found = inverse[child, z * 12 + group]
        start = pl.multiple_of(jnp.maximum(found, 0) * BS, BS)
        return found, pltpu.make_async_copy(
            every.at[child, pl.ds(start, BS)],
            row_side.at[child, pl.ds(pl.multiple_of(group * BS, BS), BS)],
            row_sems.at[child, group],
        )

    def col_copy(child, j):
        found = inverse[child, first_col + j]
        start = pl.multiple_of(jnp.maximum(found, 0) * BS, BS)
        return found, pltpu.make_async_copy(
            every.at[child, pl.ds(start, BS)], col_side.at[child, pl.ds(j * BS, BS)],
            col_sems.at[child, j],
        )

    @pl.when(q == 0)
    def _():
        for child in range(4):
            for j in range(3):
                found, copy = col_copy(child, j)

                @pl.when(found >= 0)
                def _():
                    copy.start()

                @pl.when(found < 0)
                def _():
                    col_side[child, blk(j)] = jnp.zeros((BS, BS), F32)

        def begin(group, carry):
            for child in range(4):
                found, copy = row_copy(child, group)

                @pl.when(found >= 0)
                def _():
                    copy.start()

                @pl.when(found < 0)
                def _():
                    row_side[child, pl.ds(pl.multiple_of(group * BS, BS), BS)] = jnp.zeros(
                        (BS, BS), F32
                    )

            return carry

        lax.fori_loop(0, 12, begin, 0)
        for t in range(NP):
            ranks = slice(t * RMAX, (t + 1) * RMAX)
            for j in range(3):
                head = dot3(split(facing[blk(j), ranks]), split(col_x[t, :RMAX, blk(j)]), 1, 0)
                high, low = split(-head)
                right[0, blk(t), blk(j)] = high
                right[1, blk(t), blk(j)] = low
            pivots[t : t + 1, :] = col_x[t, RMAX : RMAX + 1, :BS]
        for child in range(4):
            for j in range(3):
                found, copy = col_copy(child, j)

                @pl.when(found >= 0)
                def _():
                    copy.wait()

            high, low = split((col_side[child] * weights[child : child + 1]).T)
            right[0, blk(4 + child)] = high
            right[1, blk(4 + child)] = low

    packed = jnp.concatenate([row_x[t, q, :RMAX, :] for t in range(NP)], axis=0).T
    factors[...] = packed
    turned = bases[...].T
    spread = lax.broadcasted_iota(jnp.int32, (BS, NP * BS), 0) // RMAX == (
        lax.broadcasted_iota(jnp.int32, (BS, NP * BS), 1) // BS
    )
    heads = []
    for j in range(3):
        wide = jnp.where(spread, jnp.concatenate([turned[:, blk(j)]] * NP, axis=1), 0.0)
        heads.append(dot3(split(packed[blk(j)]), split(wide), 1, 0))
    for child in range(4):
        for j in range(3):
            found, copy = row_copy(child, q * 3 + j)

            @pl.when(found >= 0)
            def _():
                copy.wait()

    start = pl.multiple_of(q * 384, 384)
    left = [jnp.concatenate(heads, axis=0)] + [
        row_side[child, pl.ds(start, 384)] for child in range(4)
    ]
    left = split(jnp.concatenate(left, axis=1))
    out[...] = front[...] + dot3(left, (right[0], right[1]), 1, 0)


def update(inverse, every, front, weights, bases, facing, col_x, row_x):
    smem = pl.BlockSpec(memory_space=pltpu.SMEM)
    vmem = pl.BlockSpec(memory_space=pltpu.VMEM)
    return pl.pallas_call(
        update_kernel,
        grid=(4,),
        out_shape=(
            jax.ShapeDtypeStruct((1536, 384), F32),
            jax.ShapeDtypeStruct((1536, BS), F32),
            jax.ShapeDtypeStruct((NP, BS), F32),
        ),
        in_specs=[
            smem, pl.BlockSpec(memory_space=pl.ANY),
            pl.BlockSpec((384, 384), lambda i: (i, 0)), vmem,
            pl.BlockSpec((384, BS), lambda i: (i, 0)), vmem, vmem, vmem,
        ],
        out_specs=(
            pl.BlockSpec((384, 384), lambda i: (i, 0)),
            pl.BlockSpec((384, BS), lambda i: (i, 0)),
            pl.BlockSpec((NP, BS), lambda i: (0, 0)),
        ),
        scratch_shapes=[
            pltpu.VMEM((4, 1536, BS), F32),
            pltpu.VMEM((4, 384, BS), F32),
            pltpu.VMEM((2, 8 * BS, 384), BF16),
            pltpu.SemaphoreType.DMA((4, 12)),
            pltpu.SemaphoreType.DMA((4, 3)),
        ],
        compiler_params=pltpu.CompilerParams(vmem_limit_bytes=VMEM_LIMIT),
        name="update",
    )(inverse, every, front, weights, bases, facing, col_x, row_x)


def body(front, bases, ranks, child_map, child_factors, child_weights):
    blocks = ranks.shape[0]
    hit = child_map[:, None, :] == jnp.arange(blocks, dtype=jnp.int32)[None, :, None]
    order = jnp.arange(1, child_map.shape[1] + 1, dtype=jnp.int32)
    inverse = jnp.max(jnp.where(hit, order, 0), axis=2) - 1
    every, facing, col_x, row_x = sweep(
        inverse, ranks, child_weights, child_factors, front, bases
    )
    every = every.reshape(4, 4096, BS)
    out, factors, pivots = update(
        inverse, every, front, child_weights, bases, facing, col_x, row_x
    )
    return out, factors, pivots.reshape(NP * BS)


def solution(mesh):
    in_specs = (
        P("row", ("col", "sub")),
        P("row", None),
        P(),
        P(),
        P("sub", ("row", "col"), None),
        P(),
    )
    out_specs = (P("row", ("col", "sub")), P("row", None), P())
    return jax.shard_map(body, mesh=mesh, in_specs=in_specs, out_specs=out_specs, check_vma=False)
```

```python
import functools

import jax
import jax.numpy as jnp
from jax import lax
from jax.experimental import pallas as pl
from jax.experimental.pallas import tpu as pltpu
from jax.sharding import PartitionSpec as P

BS = 128
NP = 4
RMAX = 32
LEAD = NP * BS
XR = 40
MESH = pl.DeviceIdType.MESH
F32 = jnp.float32
BF16 = jnp.bfloat16
HI = lax.Precision.HIGHEST
VMEM_LIMIT = 56 * 1024 * 1024


def dot6(a, b, ca, cb):
    return lax.dot_general(
        a, b, (((ca,), (cb,)), ((), ())), precision=HI, preferred_element_type=F32
    )


def split(a):
    high = a.astype(BF16)
    return high, (a - high.astype(F32)).astype(BF16)


def dot3(a, b, ca, cb):
    one = lambda p, q: lax.dot_general(
        p, q, (((ca,), (cb,)), ((), ())), preferred_element_type=F32
    )
    return one(a[0], b[0]) + (one(a[0], b[1]) + one(a[1], b[0]))


def inverse_factor(block, nb=16):
    n = BS
    lane = lax.broadcasted_iota(jnp.int32, (1, n), 1)
    row = lax.broadcasted_iota(jnp.int32, (nb, 1), 0)
    unit = lax.broadcasted_iota(jnp.int32, (n, n), 0) == lax.broadcasted_iota(
        jnp.int32, (n, n), 1
    )
    state = jnp.concatenate([block, unit.astype(F32)], axis=1)
    done = []
    pivots = jnp.zeros((1, n), F32)
    for start in range(0, n, nb):
        head = state[:nb]
        forward = head[:, n:]
        columns = [
            jnp.broadcast_to(head[:, start + j : start + j + 1], (nb, n)) for j in range(nb)
        ]
        scale = jnp.zeros((nb, n), F32)
        for j in range(nb):
            pivot = columns[j][j : j + 1]
            inverse = 1.0 / pivot
            ratio = columns[j] * inverse
            below = jnp.where(row > j, ratio, 0.0)
            other = jnp.where(row == j, 0.0, ratio)
            forward = forward - below * forward[j : j + 1]
            head = head - jnp.concatenate([other, other], axis=1) * head[j : j + 1]
            for i in range(j + 1, nb):
                columns[i] = columns[i] - other * columns[i][j : j + 1]
            scale = jnp.where(row == j, inverse, scale)
            pivots = jnp.where(lane == start + j, pivot, pivots)
        done.append(forward * lax.sqrt(scale))
        if start + nb < n:
            solved = head * jnp.concatenate([scale, scale], axis=1)
            pieces = [solved, jnp.zeros((n - start - nb, 2 * n), F32)]
            if start:
                pieces = [jnp.zeros((start, 2 * n), F32)] + pieces
            rest = state[nb:]
            state = rest - dot6(rest[:, :n], jnp.concatenate(pieces, axis=0), 1, 0)
    return jnp.concatenate(done, axis=0), pivots


def remote(src, dst, send, recv, z, c, y):
    return pltpu.make_async_remote_copy(
        src_ref=src,
        dst_ref=dst,
        send_sem=send,
        recv_sem=recv,
        device_id=(z, c, y),
        device_id_type=MESH,
    )


def here():
    return lax.axis_index("row"), lax.axis_index("col"), lax.axis_index("sub")


PACK = BS + 8 + 3 * RMAX
LOWER = [(0, 0), (1, 0), (2, 0), (3, 0), (1, 1), (2, 1), (3, 1), (2, 2), (3, 2), (3, 3)]


def blk(i):
    return slice(i * BS, (i + 1) * BS)


def rank_limit(ranks, block):
    lane = lax.broadcasted_iota(jnp.int32, (1, BS), 1)
    limit = jnp.zeros((1, BS), jnp.int32)
    for t in range(NP):
        limit = jnp.where(lane // RMAX == t, ranks[t, block], limit)
    return (lane % RMAX < limit).astype(F32)


def sweep_kernel(
    inverse, ranks, weights, factors, front, bases,
    side_rows, side_cols, facing, col_out, row_out,
    ez, ex, cand, wx, wroot, wl, staged, mine, fpan, blead, corner, pack,
    z_send, z_recv, m_send, m_recv, l_send, l_recv, n_send, n_recv, w_send, w_recv,
    v_send, v_recv, b_send, b_recv, r_send, r_recv, t_send, t_recv,
    u_send, u_recv, k_send, k_recv, s_send, s_recv, d_send, d_recv, p_send, p_recv,
    q_send, q_recv, o_send, o_recv, c_send, c_recv, h_send, h_recv, local,
):
    z, c, y = here()
    x = c // 2
    core = c % 2
    other = 2 * x + (1 - core)
    place = c * 4 + y
    first = z == 0
    root = jnp.logical_and(first, place == 0)
    next_root = jnp.logical_and(first, place == 1)
    helping = jnp.logical_and(first, place != 0)

    def xs(step):
        return (x + step) % 4

    def ys(step):
        return (y + step) % 4

    def column(step):
        return 2 * xs(step) + core

    own_ez = pltpu.make_async_copy(factors.at[0], ez.at[z], local.at[0])
    own_front = pltpu.make_async_copy(front.at[pl.ds(0, LEAD)], fpan, local.at[1])
    own_bases = pltpu.make_async_copy(bases.at[pl.ds(0, LEAD)], blead, local.at[2])
    own_ex = pltpu.make_async_copy(ez, ex.at[:, x], local.at[3])
    own_side = pltpu.make_async_copy(mine, side_rows.at[y, :, :, core], local.at[4])
    own_facing = pltpu.make_async_copy(bases.at[pl.ds(384 * y, 384)], facing, local.at[5])
    own_ez.start()

    @pl.when(first)
    def _():
        own_front.start()
        own_bases.start()

    @pl.when(z == c)
    def _():
        own_facing.start()

    barrier = pltpu.get_barrier_semaphore()

    def greet(target):
        pl.semaphore_signal(barrier, inc=1, device_id=target, device_id_type=MESH)

    for step in range(1, 8):
        greet(((z + step) % 8, c, y))
    for step in range(1, 4):
        greet((z, column(step), y))
        greet((z, c, ys(step)))
    for step in range(4):
        greet((z, other, ys(step)))

    def greet_far(number, carry):
        greet((0, 2 * (1 + number // 4) + 1, number % 4))
        return carry

    def greet_corner(number, carry):
        greet((0, 2 * (1 + number // 3), 1 + number % 3))
        return carry

    @pl.when(root)
    def _():
        lax.fori_loop(0, 12, greet_far, 0)
        lax.fori_loop(0, 9, greet_corner, 0)

    far = jnp.logical_and(
        first, jnp.logical_and(x != 0, jnp.logical_or(core == 1, y != 0))
    )
    pl.semaphore_wait(barrier, 17 + far.astype(jnp.int32))

    def along_z(target):
        return remote(factors.at[0], ez.at[z], z_send.at[target], z_recv.at[z], target, c, y)

    def along_z_from(source):
        return remote(
            factors.at[0], ez.at[source], z_send.at[source], z_recv.at[source], source, c, y
        )

    @pl.when(z != 0)
    def _():
        along_z(0).start()

    def send_corner():
        return remote(
            front.at[pl.ds(3 * BS, BS), pl.ds(0, BS)], corner, l_send.at[0], l_recv.at[0], 0, 0, 0
        )

    @pl.when(next_root)
    def _():
        send_corner().start()

    for step in range(1, 8):
        target = (z + step) % 8

        @pl.when(target != 0)
        def _():
            along_z(target).start()

    def facing_copy(step):
        return remote(
            bases.at[pl.ds(384 * y, 384)], facing, m_send.at[step], m_recv.at[0],
            (z + step) % 8, c, y,
        )

    own_ez.wait()
    for step in range(1, 8):
        along_z_from((z + step) % 8).wait_recv()

    def choose(step):
        return remote(
            cand.at[xs(step)], wx.at[x], w_send.at[step], w_recv.at[step], z, column(step), y
        )

    def choose_from(step):
        return remote(
            cand.at[xs(step)], wx.at[xs(4 - step)], w_send.at[step], w_recv.at[step],
            z, column(step), y,
        )

    def to_root():
        piece = wroot.at[y, x, core]
        return remote(piece, piece, n_send.at[0], n_recv.at[place], 0, 0, 0)

    @pl.when(first)
    def _():
        for p in range(NP):
            found = inverse[y, p] - 1
            held = jnp.logical_and(found >= 0, found % 4 == x)
            rows = ez[jnp.maximum(found, 0) // 4]
            cand[p] = jnp.where(held, rows, 0.0)
        for step in range(1, 4):
            choose(step).start()
        total = cand[x]
        for step in range(1, 4):
            choose_from(step).wait_recv()
            total = total + wx[xs(4 - step)]
        wroot[y, x, core] = total

    @pl.when(helping)
    def _():
        to_root().start()
        to_root().wait_send()

    def over_x(step):
        return remote(ez, ex.at[:, x], b_send.at[step], b_recv.at[step], z, column(step), y)

    def over_x_from(step):
        return remote(
            ez, ex.at[:, xs(4 - step)], b_send.at[step], b_recv.at[step], z, column(step), y
        )

    own_ex.start()
    for step in range(1, 4):
        over_x(step).start()

    @pl.when(z == c)
    def _():
        for step in range(1, 8):
            facing_copy(step).start()

    def finish_x():
        own_ex.wait()
        for step in range(1, 4):
            over_x_from(step).wait_recv()

    def child_rows(group):
        found = inverse[y, group] - 1
        spot = jnp.maximum(found, 0)
        return jnp.where(found >= 0, ex[spot // 4, spot % 4], 0.0)

    def leading(step):
        piece = wl.at[y, :, core]
        return remote(piece, piece, v_send.at[step], v_recv.at[step], z, c, ys(step))

    def leading_from(step):
        piece = wl.at[ys(4 - step), :, core]
        return remote(piece, piece, v_send.at[step], v_recv.at[step], z, c, ys(step))

    def pair_leading(side):
        piece = wl.at[:, :, side]
        return remote(piece, piece, k_send.at[0], k_recv.at[0], z, other, y)

    def go_leading():
        for p in range(NP):
            wl[y, p, core] = child_rows(p)
        for step in range(1, 4):
            leading(step).start()

    def go_pair():
        for step in range(1, 4):
            leading_from(step).wait_recv()
        pair_leading(core).start()

    def route(side, step):
        return remote(
            staged.at[2 * step + side], side_cols.at[y, :, core], u_send.at[side, step],
            u_recv.at[side, step], z, 2 * x + (core + side) % 2, ys(step),
        )

    def route_from(side, step):
        return remote(
            staged.at[2 * step + side], side_cols.at[ys(4 - step), :, (core + side) % 2],
            u_send.at[side, step], u_recv.at[side, step], z,
            2 * x + (core + side) % 2, ys(step),
        )

    others = [(side, step) for step in range(4) for side in range(2) if side or step]

    def go_route():
        for j in range(3):
            side_cols[y, j, core] = child_rows(place * 3 + j)
        for side, step in others:
            target = (2 * x + (core + side) % 2) * 4 + ys(step)
            for j in range(3):
                staged[2 * step + side, j] = child_rows(target * 3 + j)
            route(side, step).start()

    def finish_route():
        for side, step in others:
            route_from(side, step).wait_recv()

    def rows_y(step):
        return remote(
            mine.at[x], side_rows.at[y, x, :, core], r_send.at[step], r_recv.at[step],
            z, c, ys(step),
        )

    def rows_y_from(step):
        return remote(
            mine.at[x], side_rows.at[ys(4 - step), x, :, core], r_send.at[step],
            r_recv.at[step], z, c, ys(step),
        )

    def rows_x(step, child):
        piece = side_rows.at[ys(child), x, :, core]
        return remote(
            piece, piece, t_send.at[step, child], t_recv.at[step, child], z, column(step), y
        )

    def rows_x_from(step, child):
        piece = side_rows.at[ys(child), xs(4 - step), :, core]
        return remote(
            piece, piece, t_send.at[step, child], t_recv.at[step, child], z, column(step), y
        )

    def to_sibling(number, src, dst):
        return remote(src, dst, s_send.at[number], s_recv.at[number], z, other, y)

    def sibling_mine():
        return to_sibling(0, mine, side_rows.at[y, :, :, core])

    def sibling_y(step):
        piece = side_rows.at[ys(4 - step), x, :, core]
        return to_sibling(step, piece, piece)

    def sibling_x(step, child):
        piece = side_rows.at[ys(child), xs(4 - step), :, core]
        return to_sibling(3 * step + child, piece, piece)

    def go_rows_y():
        for quarter in range(4):
            for k in range(3):
                mine[quarter, k] = child_rows(z * 12 + quarter * 3 + k)
        for step in range(1, 4):
            rows_y(step).start()
        own_side.start()
        sibling_mine().start()

    def go_rows_x():
        for step in range(1, 4):
            rows_y_from(step).wait_recv()
            for peer in range(1, 4):
                rows_x(peer, 4 - step).start()
            sibling_y(step).start()

    def finish_rows():
        for child in range(1, 4):
            for step in range(1, 4):
                rows_x_from(step, child).wait_recv()
                sibling_x(step, child).start()

    def down(t, target):
        return remote(
            col_out.at[t], col_out.at[t], d_send.at[t, target], d_recv.at[t], target, c, y
        )

    def direct_targets():
        yield c, c != 0
        for target in (2, 6, 1, 7):
            yield target, c != target

    def relay_targets():
        for holder, target in ((2, 4), (2, 3), (6, 5)):
            yield target, jnp.logical_and(z == holder, c != target)

    def go_down(t):
        for target, wanted in direct_targets():
            @pl.when(wanted)
            def _():
                down(t, target).start()

    def go_relay(t):
        for target, wanted in relay_targets():
            @pl.when(wanted)
            def _():
                down(t, target).start()

    def across_x(t, step):
        return remote(
            col_out.at[t], row_out.at[t, y], p_send.at[t, step], p_recv.at[t], z, column(step), y
        )

    def across_y(t, step):
        piece = row_out.at[t, y]
        return remote(piece, piece, q_send.at[t, step], q_recv.at[t, step], z, c, ys(step))

    def across_y_from(t, step):
        piece = row_out.at[t, ys(4 - step)]
        return remote(piece, piece, q_send.at[t, step], q_recv.at[t, step], z, c, ys(step))

    def across_core(t):
        piece = row_out.at[t]
        return remote(piece, piece, o_send.at[t], o_recv.at[t], z, other, y)

    def own_rows(t):
        return pltpu.make_async_copy(col_out.at[t], row_out.at[t, y], local.at[6 + t])

    def share(t):
        @pl.when(z == c)
        def _():
            own_rows(t).start()
            for step in range(1, 4):
                across_x(t, step).start()

    holds = core == z % 2

    def share_y(t):
        @pl.when(holds)
        def _():
            @pl.when(z == c)
            def _():
                own_rows(t).wait()

            @pl.when(z != c)
            def _():
                across_x(t, 1).wait_recv()

            for step in range(1, 4):
                across_y(t, step).start()

    def share_core(t):
        @pl.when(holds)
        def _():
            for step in range(1, 4):
                across_y_from(t, step).wait_recv()
            across_core(t).start()

    def pack_rows(t):
        return pack.at[t, pl.ds(0, PACK - RMAX * t)]

    def give_x(t, step):
        rows = pack_rows(t)
        return remote(rows, rows, c_send.at[t, step], c_recv.at[t], 0, column(step), y)

    def give_y(t, step):
        rows = pack_rows(t)
        return remote(rows, rows, c_send.at[t, 4 + step], c_recv.at[t], 0, c, ys(step))

    def give_sibling(t):
        rows = pack_rows(t)
        return remote(rows, rows, h_send.at[t], h_recv.at[t], z, other, y)

    def head_rows(k):
        start = BS + 8 + RMAX * (3 - k)
        return slice(start, start + RMAX)

    spreading = jnp.logical_and(first, jnp.logical_and(core == 0, y == 0))

    @pl.when(root)
    def _():
        own_bases.wait()
        masks = [blead[blk(i)] * rank_limit(ranks, i) for i in range(NP)]
        projectors = {}
        for i in range(1, NP):
            for t in range(i):
                basis = masks[i][:, t * RMAX : (t + 1) * RMAX]
                projectors[t, i] = dot6(basis, basis, 1, 1)
        own_front.wait()
        send_corner().wait_recv()
        for source in range(1, 32):
            piece = wroot.at[source % 4, source // 8, (source // 4) % 2]
            remote(piece, piece, n_send.at[0], n_recv.at[source], 0, 0, 1).wait_recv()
        plain = jnp.concatenate([wroot[s].reshape(LEAD, BS) for s in range(4)], axis=1)
        wide = jnp.concatenate(
            [wroot[s].reshape(LEAD, BS) * weights[s : s + 1] for s in range(4)], axis=1
        )
        left = dot6(wide, plain[: 2 * BS], 1, 1)
        right = dot6(wide[2 * BS :], plain[2 * BS :], 1, 1)
        state = {}
        for i, k in LOWER:
            added = left[blk(i), blk(k)] if k < 2 else right[blk(i - 2), blk(k - 2)]
            state[i, k] = (fpan[blk(i), blk(k)] if k < 3 else corner[...]) + added
        for t in range(NP):
            factor, pivots = inverse_factor(state[t, t])
            pack[t, :BS] = factor
            pack[t, BS : BS + 8] = jnp.broadcast_to(pivots, (8, BS))
            col_out[t, RMAX:] = jnp.broadcast_to(
                jnp.concatenate([pivots] * 3, axis=1), (XR - RMAX, 384)
            )
            heads = {}
            for i in range(t + 1, NP):
                solved = dot6(state[i, t], factor, 1, 1)
                packed = dot6(masks[i][:, t * RMAX : (t + 1) * RMAX], solved, 0, 1)
                pack[t, head_rows(i)] = packed
                if i < 3:
                    col_out[t, :RMAX, blk(i)] = packed
                heads[i] = dot6(solved, projectors[t, i], 1, 0)
                for k in range(t + 1, i + 1):
                    state[i, k] = state[i, k] - dot6(heads[i], heads[k], 1, 1)
            for j in range(min(t + 1, 3)):
                col_out[t, :RMAX, blk(j)] = jnp.zeros((RMAX, BS), F32)
            for step in range(1, 4):
                give_x(t, step).start()
                give_y(t, step).start()
            give_sibling(t).start()
            go_down(t)
            share(t)
            if t == 0:
                finish_x()
                go_leading()
                go_route()
                go_rows_y()
            if t == 1:
                go_pair()
                go_rows_x()
        for t in range(NP):
            share_y(t)
        pair_leading(1 - core).wait_recv()
        finish_route()
        own_facing.wait()
        for t in range(NP):
            share_core(t)
        finish_rows()
        for t in range(NP):
            for step in range(1, 4):
                give_x(t, step).wait_send()

    @pl.when(helping)
    def _():
        finish_x()
        go_leading()
        go_route()
        go_pair()
        go_rows_y()
        own_front.wait()
        own_bases.wait()

        @pl.when(z != c)
        def _():
            facing_copy(1).wait_recv()

        @pl.when(z == c)
        def _():
            own_facing.wait()

        pair_leading(1 - core).wait_recv()
        finish_route()
        plain = jnp.concatenate([wl[s].reshape(LEAD, BS) for s in range(4)], axis=1)
        wide = jnp.concatenate(
            [side_cols[s].reshape(3 * BS, BS) * weights[s : s + 1] for s in range(4)], axis=1
        )
        rows = fpan[...].T + dot3(split(wide), split(plain), 1, 1)
        masks = [facing[blk(j)] * rank_limit(ranks, place * 3 + j) for j in range(3)]
        for t in range(NP):
            @pl.when(core == 0)
            def _():
                give_x(t, 1).wait_recv()

                @pl.when(y == 0)
                def _():
                    for step in range(1, 4):
                        give_y(t, step).start()

                give_sibling(t).start()

            @pl.when(core == 1)
            def _():
                give_sibling(t).wait_recv()

            solved = dot3(split(rows[:, :BS]), split(pack[t, :BS]), 1, 1)
            spans = []
            for j in range(3):
                basis = split(masks[j][:, t * RMAX : (t + 1) * RMAX])
                part = jnp.where(place * 3 + j > t, solved[blk(j)], 0.0)
                packed = dot3(basis, split(part), 0, 1)
                col_out[t, :RMAX, blk(j)] = packed
                col_out[t, RMAX:, blk(j)] = pack[t, BS : BS + 8]
                if t + 1 < NP:
                    spans.append(dot3(split(packed), basis, 0, 1))
            go_down(t)
            share(t)
            if t + 1 < NP:
                heads = [
                    dot3(
                        split(pack[t, head_rows(k)]),
                        split(blead[blk(k), t * RMAX : (t + 1) * RMAX]), 0, 1,
                    )
                    for k in range(t + 1, NP)
                ]
                span = split(jnp.concatenate(spans, axis=0))
                later = split(jnp.concatenate(heads, axis=0))
                rows = rows[:, BS:] - dot3(span, later, 1, 1)
            if t == 1:
                go_rows_x()
        for t in range(NP):
            share_y(t)
        for t in range(NP):
            share_core(t)
        finish_rows()

    @pl.when(first)
    def _():
        pair_leading(core).wait_send()
        for step in range(1, 4):
            choose(step).wait_send()
            leading(step).wait_send()
        for t in range(NP):
            for target, wanted in direct_targets():
                @pl.when(wanted)
                def _():
                    down(t, target).wait_send()

            @pl.when(core == 0)
            def _():
                give_sibling(t).wait_send()

            @pl.when(spreading)
            def _():
                for step in range(1, 4):
                    give_y(t, step).wait_send()

    @pl.when(next_root)
    def _():
        send_corner().wait_send()

    @pl.when(jnp.logical_not(first))
    def _():
        finish_x()
        go_route()
        go_rows_y()
        go_rows_x()

        @pl.when(z != c)
        def _():
            facing_copy(1).wait_recv()

        @pl.when(z == c)
        def _():
            own_facing.wait()

        finish_route()
        finish_rows()
        for t in range(NP):
            down(t, c).wait_recv()
            go_relay(t)
            share(t)
            share_y(t)
            if t:
                share_core(t - 1)
        share_core(NP - 1)
        for t in range(NP):
            for target, wanted in relay_targets():
                @pl.when(wanted)
                def _():
                    down(t, target).wait_send()

    @pl.when(jnp.logical_not(holds))
    def _():
        for t in range(NP):
            across_core(t).wait_recv()

    @pl.when(holds)
    def _():
        for t in range(NP):
            across_core(t).wait_send()
            for step in range(1, 4):
                across_y(t, step).wait_send()

    own_side.wait()
    sibling_mine().wait()
    for step in range(1, 4):
        sibling_y(step).wait()
        for child in range(1, 4):
            sibling_x(step, child).wait()
            rows_x(step, child).wait_send()
        rows_y(step).wait_send()
        over_x(step).wait_send()
    for side, step in others:
        route(side, step).wait_send()
    for step in range(1, 8):
        along_z((z + step) % 8).wait_send()

    @pl.when(z == c)
    def _():
        for step in range(1, 8):
            facing_copy(step).wait_send()
        for t in range(NP):
            for step in range(1, 4):
                across_x(t, step).wait_send()


def sweep(inverse, ranks, weights, factors, front, bases):
    dma = pltpu.SemaphoreType.DMA
    hbm = pl.BlockSpec(memory_space=pl.ANY)
    vmem = pl.BlockSpec(memory_space=pltpu.VMEM)
    half = (64, BS)
    return pl.pallas_call(
        sweep_kernel,
        out_shape=(
            jax.ShapeDtypeStruct((4, 4, 3, 2) + half, F32),
            jax.ShapeDtypeStruct((4, 3, 2) + half, F32),
            jax.ShapeDtypeStruct((384, BS), F32),
            jax.ShapeDtypeStruct((NP, XR, 384), F32),
            jax.ShapeDtypeStruct((NP, 4, XR, 384), F32),
        ),
        in_specs=[pl.BlockSpec(memory_space=pltpu.SMEM)] * 2 + [vmem, hbm, hbm, hbm],
        out_specs=(hbm, vmem, vmem, vmem, vmem),
        scratch_shapes=[
            pltpu.VMEM((8,) + half, F32),
            pltpu.VMEM((8, 4) + half, F32),
            pltpu.VMEM((4,) + half, F32),
            pltpu.VMEM((4,) + half, F32),
            pltpu.VMEM((4, 4, 2) + half, F32),
            pltpu.VMEM((4, 4, 2) + half, F32),
            pltpu.VMEM((8, 3) + half, F32),
            pltpu.VMEM((4, 3) + half, F32),
            pltpu.VMEM((LEAD, 384), F32),
            pltpu.VMEM((LEAD, BS), F32),
            pltpu.VMEM((BS, BS), F32),
            pltpu.VMEM((NP, PACK, BS), F32),
            dma((8,)), dma((8,)), dma((8,)), dma((1,)), dma((1,)), dma((1,)),
            dma((1,)), dma((32,)), dma((4,)), dma((4,)),
            dma((4,)), dma((4,)), dma((4,)), dma((4,)), dma((4,)), dma((4,)),
            dma((4, 4)), dma((4, 4)),
            dma((2, 4)), dma((2, 4)), dma((1,)), dma((1,)), dma((16,)), dma((16,)),
            dma((NP, 8)), dma((NP,)), dma((NP, 4)), dma((NP,)),
            dma((NP, 4)), dma((NP, 4)), dma((NP,)), dma((NP,)),
            dma((NP, 8)), dma((NP,)), dma((NP,)), dma((NP,)),
            dma((10,)),
        ],
        compiler_params=pltpu.CompilerParams(
            collective_id=0, has_side_effects=True, vmem_limit_bytes=VMEM_LIMIT
        ),
        name="sweep",
    )(inverse, ranks, weights, factors, front, bases)


def update_kernel(
    side_rows, side_cols, front, weights, bases, facing, col_x, row_x, out, factors, pivots, right
):
    @pl.when(pl.program_id(0) == 0)
    def _():
        for t in range(NP):
            ranks = slice(t * RMAX, (t + 1) * RMAX)
            for j in range(3):
                head = dot3(split(facing[blk(j), ranks]), split(col_x[t, :RMAX, blk(j)]), 1, 0)
                high, low = split(-head)
                right[0, blk(t), blk(j)] = high
                right[1, blk(t), blk(j)] = low
            pivots[t : t + 1, :] = col_x[t, RMAX : RMAX + 1, :BS]
        for child in range(4):
            high, low = split((side_cols[child] * weights[child : child + 1]).T)
            right[0, blk(4 + child)] = high
            right[1, blk(4 + child)] = low

    packed = jnp.concatenate([row_x[t, 0, :RMAX, :] for t in range(NP)], axis=0).T
    factors[...] = packed
    turned = bases[...].T
    spread = lax.broadcasted_iota(jnp.int32, (BS, NP * BS), 0) // RMAX == (
        lax.broadcasted_iota(jnp.int32, (BS, NP * BS), 1) // BS
    )
    heads = []
    for j in range(3):
        wide = jnp.where(spread, jnp.concatenate([turned[:, blk(j)]] * NP, axis=1), 0.0)
        heads.append(dot3(split(packed[blk(j)]), split(wide), 1, 0))
    left = [jnp.concatenate(heads, axis=0)] + [side_rows[child] for child in range(4)]
    left = split(jnp.concatenate(left, axis=1))
    out[...] = front[...] + dot3(left, (right[0], right[1]), 1, 0)


def update(side_rows, side_cols, front, weights, bases, facing, col_x, row_x):
    vmem = pl.BlockSpec(memory_space=pltpu.VMEM)
    return pl.pallas_call(
        update_kernel,
        grid=(4,),
        out_shape=(
            jax.ShapeDtypeStruct((1536, 384), F32),
            jax.ShapeDtypeStruct((1536, BS), F32),
            jax.ShapeDtypeStruct((NP, BS), F32),
        ),
        in_specs=[
            pl.BlockSpec((4, 384, BS), lambda i: (0, i, 0)), vmem,
            pl.BlockSpec((384, 384), lambda i: (i, 0)), vmem,
            pl.BlockSpec((384, BS), lambda i: (i, 0)), vmem, vmem,
            pl.BlockSpec((NP, 1, XR, 384), lambda i: (0, i, 0, 0)),
        ],
        out_specs=(
            pl.BlockSpec((384, 384), lambda i: (i, 0)),
            pl.BlockSpec((384, BS), lambda i: (i, 0)),
            pl.BlockSpec((NP, BS), lambda i: (0, 0)),
        ),
        scratch_shapes=[pltpu.VMEM((2, 8 * BS, 384), BF16)],
        compiler_params=pltpu.CompilerParams(vmem_limit_bytes=VMEM_LIMIT),
        name="update",
    )(side_rows, side_cols, front, weights, bases, facing, col_x, row_x)


def body(front, bases, ranks, child_map, child_factors, child_weights):
    blocks = ranks.shape[0]
    hit = child_map[:, None, :] == jnp.arange(blocks, dtype=jnp.int32)[None, :, None]
    order = jnp.arange(1, child_map.shape[1] + 1, dtype=jnp.int32)
    inverse = jnp.max(jnp.where(hit, order, 0), axis=2)
    side_rows, side_cols, facing, col_x, row_x = sweep(
        inverse, ranks.T, child_weights, child_factors, front, bases
    )
    out, factors, pivots = update(
        side_rows.reshape(4, 1536, BS), side_cols.reshape(4, 384, BS), front, child_weights,
        bases, facing, col_x, row_x,
    )
    return out, factors, pivots.reshape(NP * BS)


def solution(mesh):
    in_specs = (
        P("row", ("col", "sub")),
        P("row", None),
        P(),
        P(),
        P("sub", ("row", "col"), None),
        P(),
    )
    out_specs = (P("row", ("col", "sub")), P("row", None), P())
    return jax.shard_map(body, mesh=mesh, in_specs=in_specs, out_specs=out_specs, check_vma=False)
```

```python
import functools

import jax
import jax.numpy as jnp
from jax import lax
from jax.experimental import pallas as pl
from jax.experimental.pallas import tpu as pltpu
from jax.sharding import PartitionSpec as P

BS = 128
NP = 4
RMAX = 32
LEAD = NP * BS
XR = 40
MESH = pl.DeviceIdType.MESH
F32 = jnp.float32
BF16 = jnp.bfloat16
HI = lax.Precision.HIGHEST
VMEM_LIMIT = 56 * 1024 * 1024


def dot6(a, b, ca, cb):
    return lax.dot_general(
        a, b, (((ca,), (cb,)), ((), ())), precision=HI, preferred_element_type=F32
    )


def split(a):
    high = a.astype(BF16)
    return high, (a - high.astype(F32)).astype(BF16)


def dot3(a, b, ca, cb):
    one = lambda p, q: lax.dot_general(
        p, q, (((ca,), (cb,)), ((), ())), preferred_element_type=F32
    )
    return one(a[0], b[0]) + (one(a[0], b[1]) + one(a[1], b[0]))


def inverse_factor(block, nb=16):
    n = BS
    lane = lax.broadcasted_iota(jnp.int32, (1, n), 1)
    row = lax.broadcasted_iota(jnp.int32, (nb, 1), 0)
    unit = lax.broadcasted_iota(jnp.int32, (n, n), 0) == lax.broadcasted_iota(
        jnp.int32, (n, n), 1
    )
    state = jnp.concatenate([block, unit.astype(F32)], axis=1)
    done = []
    pivots = jnp.zeros((1, n), F32)
    for start in range(0, n, nb):
        head = state[:nb]
        forward = head[:, n:]
        columns = [
            jnp.broadcast_to(head[:, start + j : start + j + 1], (nb, n)) for j in range(nb)
        ]
        scale = jnp.zeros((nb, n), F32)
        for j in range(nb):
            pivot = columns[j][j : j + 1]
            inverse = 1.0 / pivot
            ratio = columns[j] * inverse
            below = jnp.where(row > j, ratio, 0.0)
            other = jnp.where(row == j, 0.0, ratio)
            forward = forward - below * forward[j : j + 1]
            head = head - jnp.concatenate([other, other], axis=1) * head[j : j + 1]
            for i in range(j + 1, nb):
                columns[i] = columns[i] - other * columns[i][j : j + 1]
            scale = jnp.where(row == j, inverse, scale)
            pivots = jnp.where(lane == start + j, pivot, pivots)
        done.append(forward * lax.sqrt(scale))
        if start + nb < n:
            solved = head * jnp.concatenate([scale, scale], axis=1)
            pieces = [solved, jnp.zeros((n - start - nb, 2 * n), F32)]
            if start:
                pieces = [jnp.zeros((start, 2 * n), F32)] + pieces
            rest = state[nb:]
            state = rest - dot6(rest[:, :n], jnp.concatenate(pieces, axis=0), 1, 0)
    return jnp.concatenate(done, axis=0), pivots


def remote(src, dst, send, recv, z, c, y):
    return pltpu.make_async_remote_copy(
        src_ref=src,
        dst_ref=dst,
        send_sem=send,
        recv_sem=recv,
        device_id=(z, c, y),
        device_id_type=MESH,
    )


def here():
    return lax.axis_index("row"), lax.axis_index("col"), lax.axis_index("sub")


PACK = BS + 8 + 3 * RMAX
LOWER = [(0, 0), (1, 0), (2, 0), (3, 0), (1, 1), (2, 1), (3, 1), (2, 2), (3, 2), (3, 3)]


def blk(i):
    return slice(i * BS, (i + 1) * BS)


def rank_limit(ranks, block):
    lane = lax.broadcasted_iota(jnp.int32, (1, BS), 1)
    limit = jnp.zeros((1, BS), jnp.int32)
    for t in range(NP):
        limit = jnp.where(lane // RMAX == t, ranks[t, block], limit)
    return (lane % RMAX < limit).astype(F32)


def sweep_kernel(
    inverse, ranks, weights, factors, front, bases,
    side_rows, side_cols, facing, col_out, row_out,
    ez, ex, cand, wx, wroot, wl, staged, mine, fpan, blead, corner, pack,
    z_send, z_recv, m_send, m_recv, l_send, l_recv, n_send, n_recv, w_send, w_recv,
    v_send, v_recv, b_send, b_recv, r_send, r_recv, t_send, t_recv,
    u_send, u_recv, k_send, k_recv, s_send, s_recv, d_send, d_recv, p_send, p_recv,
    q_send, q_recv, o_send, o_recv, c_send, c_recv, h_send, h_recv, local,
):
    z, c, y = here()
    x = c // 2
    core = c % 2
    other = 2 * x + (1 - core)
    place = c * 4 + y
    first = z == 0
    root = jnp.logical_and(first, place == 0)
    next_root = jnp.logical_and(first, place == 1)
    helping = jnp.logical_and(first, place != 0)

    def xs(step):
        return (x + step) % 4

    def ys(step):
        return (y + step) % 4

    def column(step):
        return 2 * xs(step) + core

    own_ez = pltpu.make_async_copy(factors.at[0], ez.at[z], local.at[0])
    own_front = pltpu.make_async_copy(front.at[pl.ds(0, LEAD)], fpan, local.at[1])
    own_bases = pltpu.make_async_copy(bases.at[pl.ds(0, LEAD)], blead, local.at[2])
    own_ex = pltpu.make_async_copy(ez, ex.at[:, x], local.at[3])
    own_side = pltpu.make_async_copy(mine, side_rows.at[y, :, :, core], local.at[4])
    own_facing = pltpu.make_async_copy(bases.at[pl.ds(384 * y, 384)], facing, local.at[5])
    own_ez.start()

    @pl.when(first)
    def _():
        own_front.start()
        own_bases.start()

    @pl.when(z == c)
    def _():
        own_facing.start()

    barrier = pltpu.get_barrier_semaphore()

    def greet(target):
        pl.semaphore_signal(barrier, inc=1, device_id=target, device_id_type=MESH)

    for step in range(1, 8):
        greet(((z + step) % 8, c, y))
    for step in range(1, 4):
        greet((z, column(step), y))
        greet((z, c, ys(step)))
    for step in range(4):
        greet((z, other, ys(step)))

    def greet_far(number, carry):
        greet((0, 2 * (1 + number // 4) + 1, number % 4))
        return carry

    def greet_corner(number, carry):
        greet((0, 2 * (1 + number // 3), 1 + number % 3))
        return carry

    @pl.when(root)
    def _():
        lax.fori_loop(0, 12, greet_far, 0)
        lax.fori_loop(0, 9, greet_corner, 0)

    far = jnp.logical_and(
        first, jnp.logical_and(x != 0, jnp.logical_or(core == 1, y != 0))
    )
    pl.semaphore_wait(barrier, 17 + far.astype(jnp.int32))

    def along_z(target):
        return remote(factors.at[0], ez.at[z], z_send.at[target], z_recv.at[z], target, c, y)

    def along_z_from(source):
        return remote(
            factors.at[0], ez.at[source], z_send.at[source], z_recv.at[source], source, c, y
        )

    @pl.when(z != 0)
    def _():
        along_z(0).start()

    def send_corner():
        return remote(
            front.at[pl.ds(3 * BS, BS), pl.ds(0, BS)], corner, l_send.at[0], l_recv.at[0], 0, 0, 0
        )

    @pl.when(next_root)
    def _():
        send_corner().start()

    for step in range(1, 8):
        target = (z + step) % 8

        @pl.when(target != 0)
        def _():
            along_z(target).start()

    def facing_copy(step):
        return remote(
            bases.at[pl.ds(384 * y, 384)], facing, m_send.at[step], m_recv.at[0],
            (z + step) % 8, c, y,
        )

    own_ez.wait()
    for step in range(1, 8):
        along_z_from((z + step) % 8).wait_recv()

    def choose(step):
        return remote(
            cand.at[xs(step)], wx.at[x], w_send.at[step], w_recv.at[step], z, column(step), y
        )

    def choose_from(step):
        return remote(
            cand.at[xs(step)], wx.at[xs(4 - step)], w_send.at[step], w_recv.at[step],
            z, column(step), y,
        )

    def to_root():
        piece = wroot.at[y, x, core]
        return remote(piece, piece, n_send.at[0], n_recv.at[place], 0, 0, 0)

    @pl.when(first)
    def _():
        for p in range(NP):
            found = inverse[y, p] - 1
            held = jnp.logical_and(found >= 0, found % 4 == x)
            rows = ez[jnp.maximum(found, 0) // 4]
            cand[p] = jnp.where(held, rows, 0.0)
        for step in range(1, 4):
            choose(step).start()
        total = cand[x]
        for step in range(1, 4):
            choose_from(step).wait_recv()
            total = total + wx[xs(4 - step)]
        wroot[y, x, core] = total

    @pl.when(helping)
    def _():
        to_root().start()
        to_root().wait_send()

    def over_x(step):
        return remote(ez, ex.at[:, x], b_send.at[step], b_recv.at[step], z, column(step), y)

    def over_x_from(step):
        return remote(
            ez, ex.at[:, xs(4 - step)], b_send.at[step], b_recv.at[step], z, column(step), y
        )

    own_ex.start()
    for step in range(1, 4):
        over_x(step).start()

    @pl.when(z == c)
    def _():
        for step in range(1, 8):
            facing_copy(step).start()

    def finish_x():
        own_ex.wait()
        for step in range(1, 4):
            over_x_from(step).wait_recv()

    def child_rows(group):
        found = inverse[y, group] - 1
        spot = jnp.maximum(found, 0)
        return jnp.where(found >= 0, ex[spot // 4, spot % 4], 0.0)

    def leading(step):
        piece = wl.at[y, :, core]
        return remote(piece, piece, v_send.at[step], v_recv.at[step], z, c, ys(step))

    def leading_from(step):
        piece = wl.at[ys(4 - step), :, core]
        return remote(piece, piece, v_send.at[step], v_recv.at[step], z, c, ys(step))

    def pair_leading(side):
        piece = wl.at[:, :, side]
        return remote(piece, piece, k_send.at[0], k_recv.at[0], z, other, y)

    def go_leading():
        for p in range(NP):
            wl[y, p, core] = child_rows(p)
        for step in range(1, 4):
            leading(step).start()

    def go_pair():
        for step in range(1, 4):
            leading_from(step).wait_recv()
        pair_leading(core).start()

    def route(side, step):
        return remote(
            staged.at[2 * step + side], side_cols.at[y, :, core], u_send.at[side, step],
            u_recv.at[side, step], z, 2 * x + (core + side) % 2, ys(step),
        )

    def route_from(side, step):
        return remote(
            staged.at[2 * step + side], side_cols.at[ys(4 - step), :, (core + side) % 2],
            u_send.at[side, step], u_recv.at[side, step], z,
            2 * x + (core + side) % 2, ys(step),
        )

    others = [(side, step) for step in range(4) for side in range(2) if side or step]

    def go_route():
        for j in range(3):
            side_cols[y, j, core] = child_rows(place * 3 + j)
        for side, step in others:
            target = (2 * x + (core + side) % 2) * 4 + ys(step)
            for j in range(3):
                staged[2 * step + side, j] = child_rows(target * 3 + j)
            route(side, step).start()

    def finish_route():
        for side, step in others:
            route_from(side, step).wait_recv()

    def rows_y(step):
        return remote(
            mine.at[x], side_rows.at[y, x, :, core], r_send.at[step], r_recv.at[step],
            z, c, ys(step),
        )

    def rows_y_from(step):
        return remote(
            mine.at[x], side_rows.at[ys(4 - step), x, :, core], r_send.at[step],
            r_recv.at[step], z, c, ys(step),
        )

    def rows_x(step, child):
        piece = side_rows.at[ys(child), x, :, core]
        return remote(
            piece, piece, t_send.at[step, child], t_recv.at[step, child], z, column(step), y
        )

    def rows_x_from(step, child):
        piece = side_rows.at[ys(child), xs(4 - step), :, core]
        return remote(
            piece, piece, t_send.at[step, child], t_recv.at[step, child], z, column(step), y
        )

    def to_sibling(number, src, dst):
        return remote(src, dst, s_send.at[number], s_recv.at[number], z, other, y)

    def sibling_mine():
        return to_sibling(0, mine, side_rows.at[y, :, :, core])

    def sibling_y(step):
        piece = side_rows.at[ys(4 - step), x, :, core]
        return to_sibling(step, piece, piece)

    def sibling_x(step, child):
        piece = side_rows.at[ys(child), xs(4 - step), :, core]
        return to_sibling(3 * step + child, piece, piece)

    def go_rows_y():
        for quarter in range(4):
            for k in range(3):
                mine[quarter, k] = child_rows(z * 12 + quarter * 3 + k)
        for step in range(1, 4):
            rows_y(step).start()
        own_side.start()
        sibling_mine().start()

    def go_rows_x():
        for step in range(1, 4):
            rows_y_from(step).wait_recv()
            for peer in range(1, 4):
                rows_x(peer, 4 - step).start()
            sibling_y(step).start()

    def finish_rows():
        for child in range(1, 4):
            for step in range(1, 4):
                rows_x_from(step, child).wait_recv()
                sibling_x(step, child).start()

    def down(t, target):
        return remote(
            col_out.at[t], col_out.at[t], d_send.at[t, target], d_recv.at[t], target, c, y
        )

    def direct_targets():
        yield c, c != 0
        for target in (2, 6, 1, 7):
            yield target, c != target

    def relay_targets():
        for holder, target in ((2, 4), (2, 3), (6, 5)):
            yield target, jnp.logical_and(z == holder, c != target)

    def go_down(t):
        for target, wanted in direct_targets():
            @pl.when(wanted)
            def _():
                down(t, target).start()

    def go_relay(t):
        for target, wanted in relay_targets():
            @pl.when(wanted)
            def _():
                down(t, target).start()

    def across_x(t, step):
        return remote(
            col_out.at[t], row_out.at[t, y], p_send.at[t, step], p_recv.at[t], z, column(step), y
        )

    def across_y(t, step):
        piece = row_out.at[t, y]
        return remote(piece, piece, q_send.at[t, step], q_recv.at[t, step], z, c, ys(step))

    def across_y_from(t, step):
        piece = row_out.at[t, ys(4 - step)]
        return remote(piece, piece, q_send.at[t, step], q_recv.at[t, step], z, c, ys(step))

    def across_core(t):
        piece = row_out.at[t]
        return remote(piece, piece, o_send.at[t], o_recv.at[t], z, other, y)

    def own_rows(t):
        return pltpu.make_async_copy(col_out.at[t], row_out.at[t, y], local.at[6 + t])

    def share(t):
        @pl.when(z == c)
        def _():
            own_rows(t).start()
            for step in range(1, 4):
                across_x(t, step).start()

    holds = core == z % 2

    def share_y(t):
        @pl.when(holds)
        def _():
            @pl.when(z == c)
            def _():
                own_rows(t).wait()

            @pl.when(z != c)
            def _():
                across_x(t, 1).wait_recv()

            for step in range(1, 4):
                across_y(t, step).start()

    def share_core(t):
        @pl.when(holds)
        def _():
            for step in range(1, 4):
                across_y_from(t, step).wait_recv()
            across_core(t).start()

    def pack_rows(t):
        return pack.at[t, pl.ds(0, PACK - RMAX * t)]

    def give_x(t, step):
        rows = pack_rows(t)
        return remote(rows, rows, c_send.at[t, step], c_recv.at[t], 0, column(step), y)

    def give_y(t, step):
        rows = pack_rows(t)
        return remote(rows, rows, c_send.at[t, 4 + step], c_recv.at[t], 0, c, ys(step))

    def give_sibling(t):
        rows = pack_rows(t)
        return remote(rows, rows, h_send.at[t], h_recv.at[t], z, other, y)

    def head_rows(k):
        start = BS + 8 + RMAX * (3 - k)
        return slice(start, start + RMAX)

    hub = jnp.logical_and(core == 0, y == 0)

    def relay(t):
        @pl.when(core == 0)
        def _():
            give_x(t, 1).wait_recv()

            @pl.when(y == 0)
            def _():
                for step in range(1, 4):
                    give_y(t, step).start()

            give_sibling(t).start()

        @pl.when(core == 1)
        def _():
            give_sibling(t).wait_recv()

    spreading = jnp.logical_and(first, jnp.logical_and(core == 0, y == 0))

    @pl.when(root)
    def _():
        own_bases.wait()
        masks = [blead[blk(i)] * rank_limit(ranks, i) for i in range(NP)]
        projectors = {}
        for i in range(1, NP):
            for t in range(i):
                basis = masks[i][:, t * RMAX : (t + 1) * RMAX]
                projectors[t, i] = dot6(basis, basis, 1, 1)
        own_front.wait()
        send_corner().wait_recv()
        for source in range(1, 32):
            piece = wroot.at[source % 4, source // 8, (source // 4) % 2]
            remote(piece, piece, n_send.at[0], n_recv.at[source], 0, 0, 1).wait_recv()
        plain = jnp.concatenate([wroot[s].reshape(LEAD, BS) for s in range(4)], axis=1)
        wide = jnp.concatenate(
            [wroot[s].reshape(LEAD, BS) * weights[s : s + 1] for s in range(4)], axis=1
        )
        def assembled():
            left = dot6(wide, plain[: 2 * BS], 1, 1)
            right = dot6(wide[2 * BS :], plain[2 * BS :], 1, 1)
            for i, k in LOWER[1:]:
                added = left[blk(i), blk(k)] if k < 2 else right[blk(i - 2), blk(k - 2)]
                state[i, k] = (fpan[blk(i), blk(k)] if k < 3 else corner[...]) + added

        state = {(0, 0): fpan[:BS, :BS] + dot6(wide[:BS], plain[:BS], 1, 1)}

        def eliminate(t, i, factor, heads):
            solved = dot6(state[i, t], factor, 1, 1)
            heads[i] = dot6(solved, projectors[t, i], 1, 0)
            for k in range(t + 1, i + 1):
                state[i, k] = state[i, k] - dot6(heads[i], heads[k], 1, 1)
            packed = dot6(masks[i][:, t * RMAX : (t + 1) * RMAX], solved, 0, 1)
            pack[t, head_rows(i)] = packed
            if i < 3:
                col_out[t, :RMAX, blk(i)] = packed

        def finish_pivot(t, factor, pivots, heads):
            pack[t, :BS] = factor
            pack[t, BS : BS + 8] = jnp.broadcast_to(pivots, (8, BS))
            col_out[t, RMAX:] = jnp.broadcast_to(
                jnp.concatenate([pivots] * 3, axis=1), (XR - RMAX, 384)
            )
            for j in range(min(t + 1, 3)):
                col_out[t, :RMAX, blk(j)] = jnp.zeros((RMAX, BS), F32)
            for i in range(t + 2, NP):
                eliminate(t, i, factor, heads)
            for step in range(1, 4):
                give_x(t, step).start()
                give_y(t, step).start()
            give_sibling(t).start()
            go_down(t)
            share(t)

        pending = None
        for t in range(NP):
            factor, pivots = inverse_factor(state[t, t])
            if t == 0:
                assembled()
            if pending is not None:
                finish_pivot(*pending)
            heads = {}
            if t + 1 < NP:
                eliminate(t, t + 1, factor, heads)
            pending = (t, factor, pivots, heads)
            if t >= 2:
                finish_pivot(*pending)
                pending = None
            if t == 0:
                finish_x()
                go_leading()
                go_route()
                go_rows_y()
            if t == 2:
                go_pair()
        go_rows_x()
        for t in range(NP):
            share_y(t)
        pair_leading(1 - core).wait_recv()
        finish_route()
        own_facing.wait()
        for t in range(NP):
            share_core(t)
        finish_rows()
        for t in range(NP):
            for step in range(1, 4):
                give_x(t, step).wait_send()

    @pl.when(helping)
    def _():
        finish_x()
        go_leading()
        go_route()
        go_rows_y()
        own_front.wait()
        own_bases.wait()
        turned = fpan[...].T
        go_pair()

        @pl.when(hub)
        def _():
            relay(0)


        @pl.when(z != c)
        def _():
            facing_copy(1).wait_recv()

        @pl.when(z == c)
        def _():
            own_facing.wait()

        pair_leading(1 - core).wait_recv()
        plain = split(jnp.concatenate([wl[s].reshape(LEAD, BS) for s in range(4)], axis=1))
        masks = [facing[blk(j)] * rank_limit(ranks, place * 3 + j) for j in range(3)]
        finish_route()

        @pl.when(jnp.logical_not(hub))
        def _():
            relay(0)

        wide = jnp.concatenate(
            [side_cols[s].reshape(3 * BS, BS) * weights[s : s + 1] for s in range(4)], axis=1
        )
        rows = turned + dot3(split(wide), plain, 1, 1)
        for t in range(NP):
            if t in (0, 1):
                relay(t + 1)

            solved = dot3(split(rows[:, :BS]), split(pack[t, :BS]), 1, 1)
            spans = []
            for j in range(3):
                basis = split(masks[j][:, t * RMAX : (t + 1) * RMAX])
                part = jnp.where(place * 3 + j > t, solved[blk(j)], 0.0)
                packed = dot3(basis, split(part), 0, 1)
                col_out[t, :RMAX, blk(j)] = packed
                col_out[t, RMAX:, blk(j)] = pack[t, BS : BS + 8]
                if t + 1 < NP:
                    spans.append(dot3(split(packed), basis, 0, 1))
            go_down(t)
            share(t)
            if t + 1 < NP:
                heads = [
                    dot3(
                        split(pack[t, head_rows(k)]),
                        split(blead[blk(k), t * RMAX : (t + 1) * RMAX]), 0, 1,
                    )
                    for k in range(t + 1, NP)
                ]
                span = split(jnp.concatenate(spans, axis=0))
                later = split(jnp.concatenate(heads, axis=0))
                rows = rows[:, BS:] - dot3(span, later, 1, 1)
            if t == 2:
                relay(3)
        go_rows_x()
        for t in range(NP):
            share_y(t)
        for t in range(NP):
            share_core(t)
        finish_rows()

    @pl.when(first)
    def _():
        pair_leading(core).wait_send()
        for step in range(1, 4):
            choose(step).wait_send()
            leading(step).wait_send()
        for t in range(NP):
            for target, wanted in direct_targets():
                @pl.when(wanted)
                def _():
                    down(t, target).wait_send()

            @pl.when(core == 0)
            def _():
                give_sibling(t).wait_send()

            @pl.when(spreading)
            def _():
                for step in range(1, 4):
                    give_y(t, step).wait_send()

    @pl.when(next_root)
    def _():
        send_corner().wait_send()

    @pl.when(jnp.logical_not(first))
    def _():
        finish_x()
        go_rows_y()
        go_route()
        go_rows_x()

        @pl.when(z != c)
        def _():
            facing_copy(1).wait_recv()

        @pl.when(z == c)
        def _():
            own_facing.wait()

        finish_route()
        finish_rows()
        for t in range(NP):
            down(t, c).wait_recv()
            share(t)
            go_relay(t)
            share_y(t)
            if t:
                share_core(t - 1)
        share_core(NP - 1)
        for t in range(NP):
            for target, wanted in relay_targets():
                @pl.when(wanted)
                def _():
                    down(t, target).wait_send()

    @pl.when(jnp.logical_not(holds))
    def _():
        for t in range(NP):
            across_core(t).wait_recv()

    @pl.when(holds)
    def _():
        for t in range(NP):
            across_core(t).wait_send()
            for step in range(1, 4):
                across_y(t, step).wait_send()

    own_side.wait()
    sibling_mine().wait()
    for step in range(1, 4):
        sibling_y(step).wait()
        for child in range(1, 4):
            sibling_x(step, child).wait()
            rows_x(step, child).wait_send()
        rows_y(step).wait_send()
        over_x(step).wait_send()
    for side, step in others:
        route(side, step).wait_send()
    for step in range(1, 8):
        along_z((z + step) % 8).wait_send()

    @pl.when(z == c)
    def _():
        for step in range(1, 8):
            facing_copy(step).wait_send()
        for t in range(NP):
            for step in range(1, 4):
                across_x(t, step).wait_send()


def sweep(inverse, ranks, weights, factors, front, bases):
    dma = pltpu.SemaphoreType.DMA
    hbm = pl.BlockSpec(memory_space=pl.ANY)
    vmem = pl.BlockSpec(memory_space=pltpu.VMEM)
    half = (64, BS)
    return pl.pallas_call(
        sweep_kernel,
        out_shape=(
            jax.ShapeDtypeStruct((4, 4, 3, 2) + half, F32),
            jax.ShapeDtypeStruct((4, 3, 2) + half, F32),
            jax.ShapeDtypeStruct((384, BS), F32),
            jax.ShapeDtypeStruct((NP, XR, 384), F32),
            jax.ShapeDtypeStruct((NP, 4, XR, 384), F32),
        ),
        in_specs=[pl.BlockSpec(memory_space=pltpu.SMEM)] * 2 + [vmem, hbm, hbm, hbm],
        out_specs=(hbm, vmem, vmem, vmem, vmem),
        scratch_shapes=[
            pltpu.VMEM((8,) + half, F32),
            pltpu.VMEM((8, 4) + half, F32),
            pltpu.VMEM((4,) + half, F32),
            pltpu.VMEM((4,) + half, F32),
            pltpu.VMEM((4, 4, 2) + half, F32),
            pltpu.VMEM((4, 4, 2) + half, F32),
            pltpu.VMEM((8, 3) + half, F32),
            pltpu.VMEM((4, 3) + half, F32),
            pltpu.VMEM((LEAD, 384), F32),
            pltpu.VMEM((LEAD, BS), F32),
            pltpu.VMEM((BS, BS), F32),
            pltpu.VMEM((NP, PACK, BS), F32),
            dma((8,)), dma((8,)), dma((8,)), dma((1,)), dma((1,)), dma((1,)),
            dma((1,)), dma((32,)), dma((4,)), dma((4,)),
            dma((4,)), dma((4,)), dma((4,)), dma((4,)), dma((4,)), dma((4,)),
            dma((4, 4)), dma((4, 4)),
            dma((2, 4)), dma((2, 4)), dma((1,)), dma((1,)), dma((16,)), dma((16,)),
            dma((NP, 8)), dma((NP,)), dma((NP, 4)), dma((NP,)),
            dma((NP, 4)), dma((NP, 4)), dma((NP,)), dma((NP,)),
            dma((NP, 8)), dma((NP,)), dma((NP,)), dma((NP,)),
            dma((10,)),
        ],
        compiler_params=pltpu.CompilerParams(
            collective_id=0, has_side_effects=True, vmem_limit_bytes=VMEM_LIMIT
        ),
        name="sweep",
    )(inverse, ranks, weights, factors, front, bases)


def update_kernel(
    side_rows, side_cols, front, weights, bases, facing, col_x, row_x, out, factors, pivots, right
):
    @pl.when(pl.program_id(0) == 0)
    def _():
        for t in range(NP):
            ranks = slice(t * RMAX, (t + 1) * RMAX)
            for j in range(3):
                head = dot3(split(facing[blk(j), ranks]), split(col_x[t, :RMAX, blk(j)]), 1, 0)
                high, low = split(-head)
                right[0, blk(t), blk(j)] = high
                right[1, blk(t), blk(j)] = low
            pivots[t : t + 1, :] = col_x[t, RMAX : RMAX + 1, :BS]
        for child in range(4):
            high, low = split((side_cols[child] * weights[child : child + 1]).T)
            right[0, blk(4 + child)] = high
            right[1, blk(4 + child)] = low

    packed = jnp.concatenate([row_x[t, 0, :RMAX, :] for t in range(NP)], axis=0).T
    factors[...] = packed
    turned = bases[...].T
    spread = lax.broadcasted_iota(jnp.int32, (BS, NP * BS), 0) // RMAX == (
        lax.broadcasted_iota(jnp.int32, (BS, NP * BS), 1) // BS
    )
    heads = []
    for j in range(3):
        wide = jnp.where(spread, jnp.concatenate([turned[:, blk(j)]] * NP, axis=1), 0.0)
        heads.append(dot3(split(packed[blk(j)]), split(wide), 1, 0))
    left = [jnp.concatenate(heads, axis=0)] + [side_rows[child] for child in range(4)]
    left = split(jnp.concatenate(left, axis=1))
    out[...] = front[...] + dot3(left, (right[0], right[1]), 1, 0)


def update(side_rows, side_cols, front, weights, bases, facing, col_x, row_x):
    vmem = pl.BlockSpec(memory_space=pltpu.VMEM)
    return pl.pallas_call(
        update_kernel,
        grid=(4,),
        out_shape=(
            jax.ShapeDtypeStruct((1536, 384), F32),
            jax.ShapeDtypeStruct((1536, BS), F32),
            jax.ShapeDtypeStruct((NP, BS), F32),
        ),
        in_specs=[
            pl.BlockSpec((4, 384, BS), lambda i: (0, i, 0)), vmem,
            pl.BlockSpec((384, 384), lambda i: (i, 0)), vmem,
            pl.BlockSpec((384, BS), lambda i: (i, 0)), vmem, vmem,
            pl.BlockSpec((NP, 1, XR, 384), lambda i: (0, i, 0, 0)),
        ],
        out_specs=(
            pl.BlockSpec((384, 384), lambda i: (i, 0)),
            pl.BlockSpec((384, BS), lambda i: (i, 0)),
            pl.BlockSpec((NP, BS), lambda i: (0, 0)),
        ),
        scratch_shapes=[pltpu.VMEM((2, 8 * BS, 384), BF16)],
        compiler_params=pltpu.CompilerParams(vmem_limit_bytes=VMEM_LIMIT),
        name="update",
    )(side_rows, side_cols, front, weights, bases, facing, col_x, row_x)


def body(front, bases, ranks, child_map, child_factors, child_weights):
    blocks = ranks.shape[0]
    hit = child_map[:, None, :] == jnp.arange(blocks, dtype=jnp.int32)[None, :, None]
    order = jnp.arange(1, child_map.shape[1] + 1, dtype=jnp.int32)
    inverse = jnp.max(jnp.where(hit, order, 0), axis=2)
    side_rows, side_cols, facing, col_x, row_x = sweep(
        inverse, ranks.T, child_weights, child_factors, front, bases
    )
    out, factors, pivots = update(
        side_rows.reshape(4, 1536, BS), side_cols.reshape(4, 384, BS), front, child_weights,
        bases, facing, col_x, row_x,
    )
    return out, factors, pivots.reshape(NP * BS)


def solution(mesh):
    in_specs = (
        P("row", ("col", "sub")),
        P("row", None),
        P(),
        P(),
        P("sub", ("row", "col"), None),
        P(),
    )
    out_specs = (P("row", ("col", "sub")), P("row", None), P())
    return jax.shard_map(body, mesh=mesh, in_specs=in_specs, out_specs=out_specs, check_vma=False)
```

```python
import functools

import jax
import jax.numpy as jnp
from jax import lax
from jax.experimental import pallas as pl
from jax.experimental.pallas import tpu as pltpu
from jax.sharding import PartitionSpec as P

BS = 128
NP = 4
RMAX = 32
LEAD = NP * BS
XR = 40
MESH = pl.DeviceIdType.MESH
F32 = jnp.float32
BF16 = jnp.bfloat16
HI = lax.Precision.HIGHEST
VMEM_LIMIT = 56 * 1024 * 1024


def dot6(a, b, ca, cb):
    return lax.dot_general(
        a, b, (((ca,), (cb,)), ((), ())), precision=HI, preferred_element_type=F32
    )


def split(a):
    high = a.astype(BF16)
    return high, (a - high.astype(F32)).astype(BF16)


def dot3(a, b, ca, cb):
    one = lambda p, q: lax.dot_general(
        p, q, (((ca,), (cb,)), ((), ())), preferred_element_type=F32
    )
    return one(a[0], b[0]) + (one(a[0], b[1]) + one(a[1], b[0]))


def inverse_factor(block, nb=16):
    n = BS
    lane = lax.broadcasted_iota(jnp.int32, (1, n), 1)
    row = lax.broadcasted_iota(jnp.int32, (nb, 1), 0)
    unit = lax.broadcasted_iota(jnp.int32, (n, n), 0) == lax.broadcasted_iota(
        jnp.int32, (n, n), 1
    )
    state = jnp.concatenate([block, unit.astype(F32)], axis=1)
    done = []
    pivots = jnp.zeros((1, n), F32)
    for start in range(0, n, nb):
        head = state[:nb]
        forward = head[:, n:]
        columns = [
            jnp.broadcast_to(head[:, start + j : start + j + 1], (nb, n)) for j in range(nb)
        ]
        scale = jnp.zeros((nb, n), F32)
        for j in range(nb):
            pivot = columns[j][j : j + 1]
            inverse = 1.0 / pivot
            ratio = columns[j] * inverse
            below = jnp.where(row > j, ratio, 0.0)
            other = jnp.where(row == j, 0.0, ratio)
            forward = forward - below * forward[j : j + 1]
            head = head - jnp.concatenate([other, other], axis=1) * head[j : j + 1]
            for i in range(j + 1, nb):
                columns[i] = columns[i] - other * columns[i][j : j + 1]
            scale = jnp.where(row == j, inverse, scale)
            pivots = jnp.where(lane == start + j, pivot, pivots)
        done.append(forward * lax.sqrt(scale))
        if start + nb < n:
            solved = head * jnp.concatenate([scale, scale], axis=1)
            pieces = [solved, jnp.zeros((n - start - nb, 2 * n), F32)]
            if start:
                pieces = [jnp.zeros((start, 2 * n), F32)] + pieces
            rest = state[nb:]
            state = rest - dot6(rest[:, :n], jnp.concatenate(pieces, axis=0), 1, 0)
    return jnp.concatenate(done, axis=0), pivots


def remote(src, dst, send, recv, z, c, y):
    return pltpu.make_async_remote_copy(
        src_ref=src,
        dst_ref=dst,
        send_sem=send,
        recv_sem=recv,
        device_id=(z, c, y),
        device_id_type=MESH,
    )


def here():
    return lax.axis_index("row"), lax.axis_index("col"), lax.axis_index("sub")


PACK = BS + 8 + 3 * RMAX
LOWER = [(0, 0), (1, 0), (2, 0), (3, 0), (1, 1), (2, 1), (3, 1), (2, 2), (3, 2), (3, 3)]


def blk(i):
    return slice(i * BS, (i + 1) * BS)


def rank_limit(ranks, block):
    lane = lax.broadcasted_iota(jnp.int32, (1, BS), 1)
    limit = jnp.zeros((1, BS), jnp.int32)
    for t in range(NP):
        limit = jnp.where(lane // RMAX == t, ranks[t, block], limit)
    return (lane % RMAX < limit).astype(F32)


def sweep_kernel(
    inverse, ranks, weights, factors, front, bases,
    side_rows, side_cols, facing, col_out, row_out,
    ez, ex, cand, wx, wroot, wl, staged, mine, fpan, blead, corner, pack,
    z_send, z_recv, m_send, m_recv, l_send, l_recv, n_send, n_recv, w_send, w_recv,
    v_send, v_recv, b_send, b_recv, r_send, r_recv, t_send, t_recv,
    u_send, u_recv, k_send, k_recv, s_send, s_recv, d_send, d_recv, p_send, p_recv,
    q_send, q_recv, o_send, o_recv, c_send, c_recv, h_send, h_recv, local,
):
    z, c, y = here()
    x = c // 2
    core = c % 2
    other = 2 * x + (1 - core)
    place = c * 4 + y
    first = z == 0
    root = jnp.logical_and(first, place == 0)
    next_root = jnp.logical_and(first, place == 1)
    helping = jnp.logical_and(first, place != 0)

    def xs(step):
        return (x + step) % 4

    def ys(step):
        return (y + step) % 4

    def column(step):
        return 2 * xs(step) + core

    own_ez = pltpu.make_async_copy(factors.at[0], ez.at[z], local.at[0])
    own_front = pltpu.make_async_copy(front.at[pl.ds(0, LEAD)], fpan, local.at[1])
    own_bases = pltpu.make_async_copy(bases.at[pl.ds(0, LEAD)], blead, local.at[2])
    own_ex = pltpu.make_async_copy(ez, ex.at[:, x], local.at[3])
    own_side = pltpu.make_async_copy(mine, side_rows.at[y, :, :, core], local.at[4])
    own_facing = pltpu.make_async_copy(bases.at[pl.ds(384 * y, 384)], facing, local.at[5])
    own_ez.start()

    @pl.when(first)
    def _():
        own_front.start()
        own_bases.start()

    @pl.when(z == c)
    def _():
        own_facing.start()

    barrier = pltpu.get_barrier_semaphore()

    def greet(target):
        pl.semaphore_signal(barrier, inc=1, device_id=target, device_id_type=MESH)

    for step in range(1, 8):
        greet(((z + step) % 8, c, y))
    for step in range(1, 4):
        greet((z, column(step), y))
        greet((z, c, ys(step)))
    for step in range(4):
        greet((z, other, ys(step)))

    def greet_far(number, carry):
        greet((0, 2 * (1 + number // 4) + 1, number % 4))
        return carry

    def greet_corner(number, carry):
        greet((0, 2 * (1 + number // 3), 1 + number % 3))
        return carry

    @pl.when(root)
    def _():
        lax.fori_loop(0, 12, greet_far, 0)
        lax.fori_loop(0, 9, greet_corner, 0)

    far = jnp.logical_and(
        first, jnp.logical_and(x != 0, jnp.logical_or(core == 1, y != 0))
    )
    pl.semaphore_wait(barrier, 17 + far.astype(jnp.int32))

    def along_z(target):
        return remote(factors.at[0], ez.at[z], z_send.at[target], z_recv.at[z], target, c, y)

    def along_z_from(source):
        return remote(
            factors.at[0], ez.at[source], z_send.at[source], z_recv.at[source], source, c, y
        )

    @pl.when(z != 0)
    def _():
        along_z(0).start()

    def send_corner():
        return remote(
            front.at[pl.ds(3 * BS, BS), pl.ds(0, BS)], corner, l_send.at[0], l_recv.at[0], 0, 0, 0
        )

    @pl.when(next_root)
    def _():
        send_corner().start()

    for step in range(1, 8):
        target = (z + step) % 8

        @pl.when(target != 0)
        def _():
            along_z(target).start()

    def facing_copy(step):
        return remote(
            bases.at[pl.ds(384 * y, 384)], facing, m_send.at[step], m_recv.at[0],
            (z + step) % 8, c, y,
        )

    own_ez.wait()
    for step in range(1, 8):
        along_z_from((z + step) % 8).wait_recv()

    def choose(step):
        return remote(
            cand.at[xs(step)], wx.at[x], w_send.at[step], w_recv.at[step], z, column(step), y
        )

    def choose_from(step):
        return remote(
            cand.at[xs(step)], wx.at[xs(4 - step)], w_send.at[step], w_recv.at[step],
            z, column(step), y,
        )

    def to_root():
        piece = wroot.at[y, x, core]
        return remote(piece, piece, n_send.at[0], n_recv.at[place], 0, 0, 0)

    @pl.when(first)
    def _():
        for p in range(NP):
            found = inverse[y, p] - 1
            held = jnp.logical_and(found >= 0, found % 4 == x)
            rows = ez[jnp.maximum(found, 0) // 4]
            cand[p] = jnp.where(held, rows, 0.0)
        for step in range(1, 4):
            choose(step).start()
        total = cand[x]
        for step in range(1, 4):
            choose_from(step).wait_recv()
            total = total + wx[xs(4 - step)]
        wroot[y, x, core] = total

    @pl.when(helping)
    def _():
        to_root().start()

    def over_x(step):
        return remote(ez, ex.at[:, x], b_send.at[step], b_recv.at[step], z, column(step), y)

    def over_x_from(step):
        return remote(
            ez, ex.at[:, xs(4 - step)], b_send.at[step], b_recv.at[step], z, column(step), y
        )

    own_ex.start()
    for step in range(1, 4):
        over_x(step).start()

    @pl.when(z == c)
    def _():
        for step in range(1, 8):
            facing_copy(step).start()

    def finish_x():
        own_ex.wait()
        for step in range(1, 4):
            over_x_from(step).wait_recv()

    def child_rows(group):
        found = inverse[y, group] - 1
        spot = jnp.maximum(found, 0)
        return jnp.where(found >= 0, ex[spot // 4, spot % 4], 0.0)

    def leading(step):
        piece = wl.at[y, :, core]
        return remote(piece, piece, v_send.at[step], v_recv.at[step], z, c, ys(step))

    def leading_from(step):
        piece = wl.at[ys(4 - step), :, core]
        return remote(piece, piece, v_send.at[step], v_recv.at[step], z, c, ys(step))

    def pair_leading(side):
        piece = wl.at[:, :, side]
        return remote(piece, piece, k_send.at[0], k_recv.at[0], z, other, y)

    def go_leading():
        for p in range(NP):
            wl[y, p, core] = child_rows(p)
        for step in range(1, 4):
            leading(step).start()

    def go_pair():
        for step in range(1, 4):
            leading_from(step).wait_recv()
        pair_leading(core).start()

    def route(side, step):
        return remote(
            staged.at[2 * step + side], side_cols.at[y, :, core], u_send.at[side, step],
            u_recv.at[side, step], z, 2 * x + (core + side) % 2, ys(step),
        )

    def route_from(side, step):
        return remote(
            staged.at[2 * step + side], side_cols.at[ys(4 - step), :, (core + side) % 2],
            u_send.at[side, step], u_recv.at[side, step], z,
            2 * x + (core + side) % 2, ys(step),
        )

    others = [(side, step) for step in range(4) for side in range(2) if side or step]

    def go_route():
        for j in range(3):
            side_cols[y, j, core] = child_rows(place * 3 + j)
        for side, step in others:
            target = (2 * x + (core + side) % 2) * 4 + ys(step)
            for j in range(3):
                staged[2 * step + side, j] = child_rows(target * 3 + j)
            route(side, step).start()

    def finish_route():
        for side, step in others:
            route_from(side, step).wait_recv()

    def rows_y(step):
        return remote(
            mine.at[x], side_rows.at[y, x, :, core], r_send.at[step], r_recv.at[step],
            z, c, ys(step),
        )

    def rows_y_from(step):
        return remote(
            mine.at[x], side_rows.at[ys(4 - step), x, :, core], r_send.at[step],
            r_recv.at[step], z, c, ys(step),
        )

    def rows_x(step, child):
        piece = side_rows.at[ys(child), x, :, core]
        return remote(
            piece, piece, t_send.at[step, child], t_recv.at[step, child], z, column(step), y
        )

    def rows_x_from(step, child):
        piece = side_rows.at[ys(child), xs(4 - step), :, core]
        return remote(
            piece, piece, t_send.at[step, child], t_recv.at[step, child], z, column(step), y
        )

    def to_sibling(number, src, dst):
        return remote(src, dst, s_send.at[number], s_recv.at[number], z, other, y)

    def sibling_mine():
        return to_sibling(0, mine, side_rows.at[y, :, :, core])

    def sibling_y(step):
        piece = side_rows.at[ys(4 - step), x, :, core]
        return to_sibling(step, piece, piece)

    def sibling_x(step, child):
        piece = side_rows.at[ys(child), xs(4 - step), :, core]
        return to_sibling(3 * step + child, piece, piece)

    def go_rows_y():
        for quarter in range(4):
            for k in range(3):
                mine[quarter, k] = child_rows(z * 12 + quarter * 3 + k)
        for step in range(1, 4):
            rows_y(step).start()
        own_side.start()
        sibling_mine().start()

    def go_rows_x():
        for step in range(1, 4):
            rows_y_from(step).wait_recv()
            for peer in range(1, 4):
                rows_x(peer, 4 - step).start()
            sibling_y(step).start()

    def finish_rows():
        for child in range(1, 4):
            for step in range(1, 4):
                rows_x_from(step, child).wait_recv()
                sibling_x(step, child).start()

    def down(t, target):
        return remote(
            col_out.at[t], col_out.at[t], d_send.at[t, target], d_recv.at[t], target, c, y
        )

    def direct_targets():
        yield c, c != 0
        for target in (2, 6, 1, 7):
            yield target, c != target

    def relay_targets():
        for holder, target in ((2, 4), (2, 3), (6, 5)):
            yield target, jnp.logical_and(z == holder, c != target)

    def go_down(t):
        for target, wanted in direct_targets():
            @pl.when(wanted)
            def _():
                down(t, target).start()

    def go_relay(t):
        for target, wanted in relay_targets():
            @pl.when(wanted)
            def _():
                down(t, target).start()

    def across_x(t, step):
        return remote(
            col_out.at[t], row_out.at[t, y], p_send.at[t, step], p_recv.at[t], z, column(step), y
        )

    def across_y(t, step):
        piece = row_out.at[t, y]
        return remote(piece, piece, q_send.at[t, step], q_recv.at[t, step], z, c, ys(step))

    def across_y_from(t, step):
        piece = row_out.at[t, ys(4 - step)]
        return remote(piece, piece, q_send.at[t, step], q_recv.at[t, step], z, c, ys(step))

    def across_core(t):
        piece = row_out.at[t]
        return remote(piece, piece, o_send.at[t], o_recv.at[t], z, other, y)

    def own_rows(t):
        return pltpu.make_async_copy(col_out.at[t], row_out.at[t, y], local.at[6 + t])

    def share(t):
        @pl.when(z == c)
        def _():
            own_rows(t).start()
            for step in range(1, 4):
                across_x(t, step).start()

    holds = core == z % 2

    def share_y(t):
        @pl.when(holds)
        def _():
            @pl.when(z == c)
            def _():
                own_rows(t).wait()

            @pl.when(z != c)
            def _():
                across_x(t, 1).wait_recv()

            for step in range(1, 4):
                across_y(t, step).start()

    def share_core(t):
        @pl.when(holds)
        def _():
            for step in range(1, 4):
                across_y_from(t, step).wait_recv()
            across_core(t).start()

    def pack_rows(t):
        return pack.at[t, pl.ds(0, PACK - RMAX * t)]

    def give_x(t, step):
        rows = pack_rows(t)
        return remote(rows, rows, c_send.at[t, step], c_recv.at[t], 0, column(step), y)

    def give_y(t, step):
        rows = pack_rows(t)
        return remote(rows, rows, c_send.at[t, 4 + step], c_recv.at[t], 0, c, ys(step))

    def give_sibling(t):
        rows = pack_rows(t)
        return remote(rows, rows, h_send.at[t], h_recv.at[t], z, other, y)

    def head_rows(k):
        start = BS + 8 + RMAX * (3 - k)
        return slice(start, start + RMAX)

    hub = jnp.logical_and(core == 0, y == 0)

    def relay(t):
        @pl.when(core == 0)
        def _():
            give_x(t, 1).wait_recv()

            @pl.when(y == 0)
            def _():
                for step in range(1, 4):
                    give_y(t, step).start()

            give_sibling(t).start()

        @pl.when(core == 1)
        def _():
            give_sibling(t).wait_recv()

    spreading = jnp.logical_and(first, jnp.logical_and(core == 0, y == 0))

    @pl.when(root)
    def _():
        own_bases.wait()
        masks = [blead[blk(i)] * rank_limit(ranks, i) for i in range(NP)]
        projectors = {}
        for i in range(1, NP):
            for t in range(i):
                basis = masks[i][:, t * RMAX : (t + 1) * RMAX]
                projectors[t, i] = dot6(basis, basis, 1, 1)
        own_front.wait()
        send_corner().wait_recv()
        for source in range(1, 32):
            piece = wroot.at[source % 4, source // 8, (source // 4) % 2]
            remote(piece, piece, n_send.at[0], n_recv.at[source], 0, 0, 1).wait_recv()
        plain = jnp.concatenate([wroot[s].reshape(LEAD, BS) for s in range(4)], axis=1)
        wide = jnp.concatenate(
            [wroot[s].reshape(LEAD, BS) * weights[s : s + 1] for s in range(4)], axis=1
        )
        def assembled():
            left = dot6(wide, plain[: 2 * BS], 1, 1)
            right = dot6(wide[2 * BS :], plain[2 * BS :], 1, 1)
            for i, k in LOWER[1:]:
                added = left[blk(i), blk(k)] if k < 2 else right[blk(i - 2), blk(k - 2)]
                state[i, k] = (fpan[blk(i), blk(k)] if k < 3 else corner[...]) + added

        state = {(0, 0): fpan[:BS, :BS] + dot6(wide[:BS], plain[:BS], 1, 1)}

        def eliminate(t, i, factor, heads):
            solved = dot6(state[i, t], factor, 1, 1)
            heads[i] = dot6(solved, projectors[t, i], 1, 0)
            for k in range(t + 1, i + 1):
                state[i, k] = state[i, k] - dot6(heads[i], heads[k], 1, 1)
            packed = dot6(masks[i][:, t * RMAX : (t + 1) * RMAX], solved, 0, 1)
            pack[t, head_rows(i)] = packed
            if i < 3:
                col_out[t, :RMAX, blk(i)] = packed

        def finish_pivot(t, factor, pivots, heads):
            pack[t, :BS] = factor
            pack[t, BS : BS + 8] = jnp.broadcast_to(pivots, (8, BS))
            col_out[t, RMAX:] = jnp.broadcast_to(
                jnp.concatenate([pivots] * 3, axis=1), (XR - RMAX, 384)
            )
            for j in range(min(t + 1, 3)):
                col_out[t, :RMAX, blk(j)] = jnp.zeros((RMAX, BS), F32)
            for i in range(t + 2, NP):
                eliminate(t, i, factor, heads)
            for step in range(1, 4):
                give_x(t, step).start()
                give_y(t, step).start()
            give_sibling(t).start()
            go_down(t)
            share(t)

        pending = None
        for t in range(NP):
            factor, pivots = inverse_factor(state[t, t])
            if t == 0:
                assembled()
            if pending is not None:
                finish_pivot(*pending)
            heads = {}
            if t + 1 < NP:
                eliminate(t, t + 1, factor, heads)
            pending = (t, factor, pivots, heads)
            if t >= 2:
                finish_pivot(*pending)
                pending = None
            if t == 0:
                finish_x()
                go_leading()
                go_route()
                go_rows_y()
            if t == 2:
                go_pair()
        go_rows_x()
        for t in range(NP):
            share_y(t)
        pair_leading(1 - core).wait_recv()
        finish_route()
        own_facing.wait()
        for t in range(NP):
            share_core(t)
        finish_rows()
        for t in range(NP):
            for step in range(1, 4):
                give_x(t, step).wait_send()

    @pl.when(helping)
    def _():
        finish_x()
        go_leading()
        go_route()
        go_rows_y()
        own_front.wait()
        own_bases.wait()
        turned = fpan[...].T
        go_pair()

        @pl.when(hub)
        def _():
            relay(0)


        @pl.when(z != c)
        def _():
            facing_copy(1).wait_recv()

        @pl.when(z == c)
        def _():
            own_facing.wait()

        pair_leading(1 - core).wait_recv()
        plain = split(jnp.concatenate([wl[s].reshape(LEAD, BS) for s in range(4)], axis=1))
        masks = [facing[blk(j)] * rank_limit(ranks, place * 3 + j) for j in range(3)]
        spans_of = {}
        for t in range(NP - 1):
            for j in range(3):
                basis = split(masks[j][:, t * RMAX : (t + 1) * RMAX])
                spans_of[t, j] = split(dot3(basis, basis, 1, 1))
        finish_route()

        @pl.when(jnp.logical_not(hub))
        def _():
            relay(0)

        wide = jnp.concatenate(
            [side_cols[s].reshape(3 * BS, BS) * weights[s : s + 1] for s in range(4)], axis=1
        )
        rows = turned + dot3(split(wide), plain, 1, 1)
        for t in range(NP):
            if t in (0, 1):
                relay(t + 1)

            solved = dot3(split(rows[:, :BS]), split(pack[t, :BS]), 1, 1)
            spans = []
            for j in range(3):
                basis = split(masks[j][:, t * RMAX : (t + 1) * RMAX])
                part = split(jnp.where(place * 3 + j > t, solved[blk(j)], 0.0))
                packed = dot3(basis, part, 0, 1)
                col_out[t, :RMAX, blk(j)] = packed
                col_out[t, RMAX:, blk(j)] = pack[t, BS : BS + 8]
                if t + 1 < NP:
                    spans.append(dot3(part, spans_of[t, j], 1, 0))
            go_down(t)
            share(t)
            if t + 1 < NP:
                heads = [
                    dot3(
                        split(pack[t, head_rows(k)]),
                        split(blead[blk(k), t * RMAX : (t + 1) * RMAX]), 0, 1,
                    )
                    for k in range(t + 1, NP)
                ]
                span = split(jnp.concatenate(spans, axis=0))
                later = split(jnp.concatenate(heads, axis=0))
                rows = rows[:, BS:] - dot3(span, later, 1, 1)
            if t == 2:
                relay(3)
        go_rows_x()
        for t in range(NP):
            share_y(t)
        for t in range(NP):
            share_core(t)
        finish_rows()

    @pl.when(first)
    def _():
        pair_leading(core).wait_send()
        for step in range(1, 4):
            choose(step).wait_send()
            leading(step).wait_send()
        for t in range(NP):
            for target, wanted in direct_targets():
                @pl.when(wanted)
                def _():
                    down(t, target).wait_send()

            @pl.when(core == 0)
            def _():
                give_sibling(t).wait_send()

            @pl.when(spreading)
            def _():
                for step in range(1, 4):
                    give_y(t, step).wait_send()

    @pl.when(helping)
    def _():
        to_root().wait_send()

    @pl.when(next_root)
    def _():
        send_corner().wait_send()

    @pl.when(jnp.logical_not(first))
    def _():
        finish_x()
        go_rows_y()
        go_route()
        go_rows_x()

        @pl.when(z != c)
        def _():
            facing_copy(1).wait_recv()

        @pl.when(z == c)
        def _():
            own_facing.wait()

        finish_route()
        finish_rows()
        for t in range(NP):
            down(t, c).wait_recv()
            share(t)
            go_relay(t)
            share_y(t)
            if t:
                share_core(t - 1)
        share_core(NP - 1)
        for t in range(NP):
            for target, wanted in relay_targets():
                @pl.when(wanted)
                def _():
                    down(t, target).wait_send()

    @pl.when(jnp.logical_not(holds))
    def _():
        for t in range(NP):
            across_core(t).wait_recv()

    @pl.when(holds)
    def _():
        for t in range(NP):
            across_core(t).wait_send()
            for step in range(1, 4):
                across_y(t, step).wait_send()

    own_side.wait()
    sibling_mine().wait()
    for step in range(1, 4):
        sibling_y(step).wait()
        for child in range(1, 4):
            sibling_x(step, child).wait()
            rows_x(step, child).wait_send()
        rows_y(step).wait_send()
        over_x(step).wait_send()
    for side, step in others:
        route(side, step).wait_send()
    for step in range(1, 8):
        along_z((z + step) % 8).wait_send()

    @pl.when(z == c)
    def _():
        for step in range(1, 8):
            facing_copy(step).wait_send()
        for t in range(NP):
            for step in range(1, 4):
                across_x(t, step).wait_send()


def sweep(inverse, ranks, weights, factors, front, bases):
    dma = pltpu.SemaphoreType.DMA
    hbm = pl.BlockSpec(memory_space=pl.ANY)
    vmem = pl.BlockSpec(memory_space=pltpu.VMEM)
    half = (64, BS)
    return pl.pallas_call(
        sweep_kernel,
        out_shape=(
            jax.ShapeDtypeStruct((4, 4, 3, 2) + half, F32),
            jax.ShapeDtypeStruct((4, 3, 2) + half, F32),
            jax.ShapeDtypeStruct((384, BS), F32),
            jax.ShapeDtypeStruct((NP, XR, 384), F32),
            jax.ShapeDtypeStruct((NP, 4, XR, 384), F32),
        ),
        in_specs=[pl.BlockSpec(memory_space=pltpu.SMEM)] * 2 + [vmem, hbm, hbm, hbm],
        out_specs=(hbm, vmem, vmem, vmem, vmem),
        scratch_shapes=[
            pltpu.VMEM((8,) + half, F32),
            pltpu.VMEM((8, 4) + half, F32),
            pltpu.VMEM((4,) + half, F32),
            pltpu.VMEM((4,) + half, F32),
            pltpu.VMEM((4, 4, 2) + half, F32),
            pltpu.VMEM((4, 4, 2) + half, F32),
            pltpu.VMEM((8, 3) + half, F32),
            pltpu.VMEM((4, 3) + half, F32),
            pltpu.VMEM((LEAD, 384), F32),
            pltpu.VMEM((LEAD, BS), F32),
            pltpu.VMEM((BS, BS), F32),
            pltpu.VMEM((NP, PACK, BS), F32),
            dma((8,)), dma((8,)), dma((8,)), dma((1,)), dma((1,)), dma((1,)),
            dma((1,)), dma((32,)), dma((4,)), dma((4,)),
            dma((4,)), dma((4,)), dma((4,)), dma((4,)), dma((4,)), dma((4,)),
            dma((4, 4)), dma((4, 4)),
            dma((2, 4)), dma((2, 4)), dma((1,)), dma((1,)), dma((16,)), dma((16,)),
            dma((NP, 8)), dma((NP,)), dma((NP, 4)), dma((NP,)),
            dma((NP, 4)), dma((NP, 4)), dma((NP,)), dma((NP,)),
            dma((NP, 8)), dma((NP,)), dma((NP,)), dma((NP,)),
            dma((10,)),
        ],
        compiler_params=pltpu.CompilerParams(
            collective_id=0, has_side_effects=True, vmem_limit_bytes=VMEM_LIMIT
        ),
        name="sweep",
    )(inverse, ranks, weights, factors, front, bases)


def update_kernel(
    side_rows, side_cols, front, weights, bases, facing, col_x, row_x, out, factors, pivots, right
):
    @pl.when(pl.program_id(0) == 0)
    def _():
        for t in range(NP):
            ranks = slice(t * RMAX, (t + 1) * RMAX)
            for j in range(3):
                head = dot3(split(facing[blk(j), ranks]), split(col_x[t, :RMAX, blk(j)]), 1, 0)
                high, low = split(-head)
                right[0, blk(t), blk(j)] = high
                right[1, blk(t), blk(j)] = low
            pivots[t : t + 1, :] = col_x[t, RMAX : RMAX + 1, :BS]
        for child in range(4):
            high, low = split((side_cols[child] * weights[child : child + 1]).T)
            right[0, blk(4 + child)] = high
            right[1, blk(4 + child)] = low

    packed = jnp.concatenate([row_x[t, 0, :RMAX, :] for t in range(NP)], axis=0).T
    factors[...] = packed
    turned = bases[...].T
    spread = lax.broadcasted_iota(jnp.int32, (BS, NP * BS), 0) // RMAX == (
        lax.broadcasted_iota(jnp.int32, (BS, NP * BS), 1) // BS
    )
    heads = []
    for j in range(3):
        wide = jnp.where(spread, jnp.concatenate([turned[:, blk(j)]] * NP, axis=1), 0.0)
        heads.append(dot3(split(packed[blk(j)]), split(wide), 1, 0))
    left = [jnp.concatenate(heads, axis=0)] + [side_rows[child] for child in range(4)]
    left = split(jnp.concatenate(left, axis=1))
    out[...] = front[...] + dot3(left, (right[0], right[1]), 1, 0)


def update(side_rows, side_cols, front, weights, bases, facing, col_x, row_x):
    vmem = pl.BlockSpec(memory_space=pltpu.VMEM)
    return pl.pallas_call(
        update_kernel,
        grid=(4,),
        out_shape=(
            jax.ShapeDtypeStruct((1536, 384), F32),
            jax.ShapeDtypeStruct((1536, BS), F32),
            jax.ShapeDtypeStruct((NP, BS), F32),
        ),
        in_specs=[
            pl.BlockSpec((4, 384, BS), lambda i: (0, i, 0)), vmem,
            pl.BlockSpec((384, 384), lambda i: (i, 0)), vmem,
            pl.BlockSpec((384, BS), lambda i: (i, 0)), vmem, vmem,
            pl.BlockSpec((NP, 1, XR, 384), lambda i: (0, i, 0, 0)),
        ],
        out_specs=(
            pl.BlockSpec((384, 384), lambda i: (i, 0)),
            pl.BlockSpec((384, BS), lambda i: (i, 0)),
            pl.BlockSpec((NP, BS), lambda i: (0, 0)),
        ),
        scratch_shapes=[pltpu.VMEM((2, 8 * BS, 384), BF16)],
        compiler_params=pltpu.CompilerParams(vmem_limit_bytes=VMEM_LIMIT),
        name="update",
    )(side_rows, side_cols, front, weights, bases, facing, col_x, row_x)


def body(front, bases, ranks, child_map, child_factors, child_weights):
    blocks = ranks.shape[0]
    hit = child_map[:, None, :] == jnp.arange(blocks, dtype=jnp.int32)[None, :, None]
    order = jnp.arange(1, child_map.shape[1] + 1, dtype=jnp.int32)
    inverse = jnp.max(jnp.where(hit, order, 0), axis=2)
    side_rows, side_cols, facing, col_x, row_x = sweep(
        inverse, ranks.T, child_weights, child_factors, front, bases
    )
    out, factors, pivots = update(
        side_rows.reshape(4, 1536, BS), side_cols.reshape(4, 384, BS), front, child_weights,
        bases, facing, col_x, row_x,
    )
    return out, factors, pivots.reshape(NP * BS)


def solution(mesh):
    in_specs = (
        P("row", ("col", "sub")),
        P("row", None),
        P(),
        P(),
        P("sub", ("row", "col"), None),
        P(),
    )
    out_specs = (P("row", ("col", "sub")), P("row", None), P())
    return jax.shard_map(body, mesh=mesh, in_specs=in_specs, out_specs=out_specs, check_vma=False)
```
